512 devices in a mesh: wide: 64 (over z, y), clus: 8 (over x, core).
Axes of the slice: x: 4, y: 4, z: 16, core: 2. Of those that a mesh axis runs over, the one named last changes fastest.
Arguments:
- duals: bfloat16 [96, 1024, 3840], P(None, ('wide', 'clus')), may hold values from -6 to 6
- kernel: bfloat16 [1024, 6, 3840], P(('wide', 'clus')), may hold values from -0.29882812 to 0.29882812
- sub_counts: int32 [512], P(('wide', 'clus')), may hold values from 1 to 2, as said below
- dual_sizes: int32 [1024], P(('wide', 'clus')), may hold values from 1920 to 3840, as said below
- cluster_factor: float32 [64, 96, 96], P('wide'), as said below
- coarse_map: int32 [64, 96], P('wide'), may hold values from 0 to 1535, as said below
- coarse_inverse: float32 [1536, 1536], P(None, 'clus'), as said below
Outputs:
- projected: bfloat16 [96, 1024, 3840], P(None, ('wide', 'clus'))
The draws below stay inside these ranges and needn't reach their ends.
Inputs may be any that keep to these rules, and one draw needn't show every extreme that they name: `sub_counts`: each device holds 1 to 2 subdomains; some device holds 2. `dual_sizes`: some slot has the full 3840. `coarse_map`: the rows of cluster w map into the 48 global rows that begin at w * 24, counted modulo 1536. `cluster_factor`: lower triangular with diagonal entries between 1 and 2. `coarse_inverse`: diagonal entries between 1 and 2.
All inputs are finite; a program needn't handle non-finite values.
Results may differ from the reference program's by a relative error of at most 0.0018.
Values sent between devices are 32-bit elements; how exact they have to be, the bound alone decides.
A program may use at most 64 MiB of HBM per device.

```python
import math
import jax
import jax.numpy as jnp
from jax import lax

DUAL = 3840
MODES = 6
SUB = 2
RHS = 96
BAND = 24
DEVS = 512
NSUB = 1024
CK = 96
GK = 1536
N_WIDE = 64
N_CLUS = 8


def draw_sub_counts(key, part):
    first_key, second_key = jax.random.split(key)
    values = jax.random.randint(first_key, (DEVS,), 1, SUB + 1)
    where_full = jax.random.randint(second_key, (), 0, DEVS)
    return values.at[where_full].set(SUB).astype(jnp.int32)


def draw_dual_sizes(key, part):
    first_key, second_key = jax.random.split(key)
    values = jax.random.randint(first_key, (NSUB,), DUAL // 2, DUAL + 1)
    where_full = jax.random.randint(second_key, (), 0, NSUB)
    return values.at[where_full].set(DUAL).astype(jnp.int32)


def draw_coarse_map(key, part):
    clusters = GK // BAND
    offsets = jax.random.randint(key, (clusters, CK), 0, 2 * BAND)
    base_rows = jnp.arange(clusters, dtype=jnp.int32)[:, None] * BAND
    mapped = (base_rows + offsets) % GK
    mapped = mapped.at[:, 0].set(base_rows[:, 0] + BAND - 1)
    mapped = mapped.at[:, 1].set(base_rows[:, 0])
    return mapped.astype(jnp.int32)


def draw_cluster_factor(key, part):
    clusters = GK // BAND
    first_key, second_key = jax.random.split(key)
    diag_vals = jnp.exp(jax.random.uniform(first_key, (clusters, CK), jnp.float32, 0.0, math.log(2.0)))
    off_vals = jax.random.uniform(second_key, (clusters, CK, CK), jnp.float32, -1.0, 1.0) * (0.8 / math.sqrt(CK))
    identity = jnp.eye(CK, dtype=jnp.float32)
    return (jnp.tril(off_vals, -1) + identity[None, :, :] * diag_vals[:, :, None]).astype(jnp.float32)


def draw_coarse_inverse(key, part):
    first_key, second_key = jax.random.split(key)
    diag_vals = jnp.exp(jax.random.uniform(first_key, (GK,), jnp.float32, 0.0, math.log(2.0)))
    off_vals = jax.random.uniform(second_key, (GK, GK), jnp.float32, -1.0, 1.0) * (0.8 / math.sqrt(GK))
    identity = jnp.eye(GK, dtype=jnp.float32)
    return (off_vals * (1.0 - identity) + identity * diag_vals[:, None]).astype(jnp.float32)


def levels(key, dims, pieces, smallest, largest):
    gain = 1.0
    for dim, parts in pieces:
        steps = jax.random.uniform(jax.random.fold_in(jax.random.fold_in(key, 6), dim), (parts,), jnp.float32, smallest / len(pieces), largest / len(pieces))
        gain = gain * jnp.repeat(jnp.exp(steps), dims[dim] // parts).reshape((-1,) + (1,) * (len(dims) - 1 - dim))
    return gain


def normal_values(stream_key, shape, width, bound, cuts=(), kind=jnp.bfloat16):
    factor_of = levels(stream_key, shape, cuts, -0.22, 0.18) if cuts else 1.0
    result = jax.random.normal(stream_key, shape, jnp.float32) * width * factor_of
    return jnp.minimum(jnp.maximum(result, -bound), bound).astype(kind)


def setup_inputs(seed: int = 0) -> dict:
    arg_keys = jax.random.split(jax.random.key(seed), 8)
    duals = normal_values(arg_keys[0], (RHS, NSUB, DUAL), 1.0, 6.0, ((1, 512),))
    kernel = normal_values(arg_keys[1], (NSUB, MODES, DUAL), 0.05, 0.29882812, ((0, 512),))
    sub_counts = draw_sub_counts(jax.random.fold_in(arg_keys[7], 71), 0)
    dual_sizes = draw_dual_sizes(jax.random.fold_in(arg_keys[7], 71), 0)
    cluster_factor = draw_cluster_factor(jax.random.fold_in(arg_keys[7], 71), 0)
    coarse_map = draw_coarse_map(jax.random.fold_in(arg_keys[7], 71), 0)
    coarse_inverse = draw_coarse_inverse(jax.random.fold_in(arg_keys[7], 71), 0)
    return dict(duals=duals, kernel=kernel, sub_counts=sub_counts, dual_sizes=dual_sizes, cluster_factor=cluster_factor, coarse_map=coarse_map, coarse_inverse=coarse_inverse)


def masked_kernel(kernel, sub_counts, dual_sizes):
    total = kernel.shape[0]
    position = lax.broadcasted_iota(jnp.int32, (total, DUAL), 1)
    slot_index = lax.broadcasted_iota(jnp.int32, (total, DUAL), 0)
    owner_count = sub_counts[slot_index // SUB]
    active = (position < dual_sizes[:, None]) & (slot_index % SUB < owner_count)
    return jnp.where(active[:, None, :], kernel, jnp.zeros_like(kernel)).astype(jnp.bfloat16)

def reference(duals, kernel, sub_counts, dual_sizes, cluster_factor, coarse_map, coarse_inverse):
    masked = masked_kernel(kernel, sub_counts, dual_sizes)
    per_cluster = SUB * N_CLUS
    hi = lax.Precision.HIGHEST

    def first(cluster):
        block = lax.dynamic_slice_in_dim(duals, cluster * per_cluster, per_cluster, 1)
        kblock = lax.dynamic_slice_in_dim(masked, cluster * per_cluster, per_cluster, 0)
        local = jnp.einsum('rsi,ski->rsk', block.astype(jnp.float32), kblock.astype(jnp.float32), precision=hi)
        local = local.reshape(RHS, CK)
        return lax.linalg.triangular_solve(cluster_factor[cluster], local.T, left_side=True, lower=True).T
    forward = lax.map(first, jnp.arange(N_WIDE, dtype=jnp.int32))
    flat = jnp.transpose(forward, (0, 2, 1)).reshape(N_WIDE * CK, RHS)
    gsum = jax.ops.segment_sum(flat, coarse_map.reshape(-1), num_segments=GK).T
    beta = jnp.dot(gsum, coarse_inverse, precision=hi)

    def second(cluster):
        block = lax.dynamic_slice_in_dim(duals, cluster * per_cluster, per_cluster, 1)
        kblock = lax.dynamic_slice_in_dim(masked, cluster * per_cluster, per_cluster, 0)
        back = beta[:, coarse_map[cluster]]
        corr = lax.linalg.triangular_solve(cluster_factor[cluster], (forward[cluster] - back).T, left_side=True, lower=True, transpose_a=True).T
        corr = corr.reshape(RHS, per_cluster, MODES).astype(jnp.bfloat16)
        delta = jnp.einsum('rsk,ski->rsi', corr.astype(jnp.float32), kblock.astype(jnp.float32), precision=hi)
        return (block.astype(jnp.float32) - delta).astype(jnp.bfloat16)
    blocks = lax.map(second, jnp.arange(N_WIDE, dtype=jnp.int32))
    return jnp.transpose(blocks, (1, 0, 2, 3)).reshape(RHS, NSUB, DUAL)
```

```python
import functools

import jax
import jax.numpy as jnp
from jax import lax
from jax.experimental import pallas as pl
from jax.experimental.pallas import tpu as pltpu
from jax.sharding import PartitionSpec as P

MESH = pl.DeviceIdType.MESH
NZ, NY, NT = 16, 4, 8
NW = NZ * NY
BAND = 24
GK = NW * BAND
CK = 96
RHS = 96
LANES = 128


def mm(a, b, dims=((1,), (0,))):
    return lax.dot_general(
        a, b, (dims, ((), ())), precision=lax.Precision.HIGHEST, preferred_element_type=jnp.float32
    )


def lower_inverse(lower):
    n = lower.shape[0]
    blocks = n // 8
    l3 = lower.reshape(blocks, 8, n)
    bi = lax.broadcasted_iota(jnp.int32, (blocks, 8, n), 0)
    ri = lax.broadcasted_iota(jnp.int32, (blocks, 8, n), 1)
    ci = lax.broadcasted_iota(jnp.int32, (blocks, 8, n), 2)
    own = ci - 8 * bi
    x = jnp.where(own == ri, 1.0, 0.0)
    rdiag = 1.0 / jnp.sum(jnp.where(own == ri, l3, 0.0), axis=2, keepdims=True)
    row = lax.broadcasted_iota(jnp.int32, (blocks, 8, 1), 1)
    for j in range(8):
        col = jnp.sum(jnp.where(own == j, l3, 0.0), axis=2, keepdims=True)
        pivot = x[:, j : j + 1, :] * rdiag[:, j : j + 1, :]
        x = jnp.where(row == j, pivot, x - jnp.where(row > j, col, 0.0) * pivot)
    x = x.reshape(n, n)
    r2 = lax.broadcasted_iota(jnp.int32, (n, n), 0)
    c2 = lax.broadcasted_iota(jnp.int32, (n, n), 1)
    size = 8
    while size < n:
        pair = 2 * size
        off = (r2 // pair == c2 // pair) & (r2 % pair >= size) & (c2 % pair < size)
        x = x - mm(x, mm(jnp.where(off, lower, 0.0), x))
        size = pair
    return x


def coarse_kernel(
    yl, low, cmap, ct, out,
    ysend, yall, gsec, gprev, cst, cpk, c48, gbuf, part, crecv,
    lsem, y_s, y_r, g_s, g_r, c_s, c_r, z_s, z_r, v_s, v_r, d_s, d_r,
):
    w = lax.axis_index("wide")
    t = lax.axis_index("clus")
    z, y = w // NY, w % NY
    wn, wp = (w + 1) % NW, (w + NW - 1) % NW
    root_n = (wn // NY) % NT
    is_root = t == z % NT
    zh = z // NT
    cs0, cs1 = w // NT, wn // NT

    def at(ww, tt):
        return (ww, tt)

    def zdev(zz):
        return (zz * NY + y, t)

    @pl.when(t == cs0)
    def _():
        pltpu.make_async_copy(
            ct.at[pl.ds(pl.multiple_of((w % NT) * BAND, 8), BAND)], cst.at[0], lsem.at[0]
        ).start()

    @pl.when(t == cs1)
    def _():
        pltpu.make_async_copy(
            ct.at[pl.ds(pl.multiple_of((wn % NT) * BAND, 8), BAND)], cst.at[1], lsem.at[1]
        ).start()

    gbuf[...] = jnp.zeros_like(gbuf)
    barrier = pltpu.get_barrier_semaphore()

    def greet(dev):
        pl.semaphore_signal(barrier, inc=1, device_id=dev, device_id_type=MESH)

    for k in range(1, NT):
        greet(at(w, (t + k) % NT))
    for k in range(1, NY):
        greet((z * NY + (y + k) % NY, t))
    greet(at(wn, root_n))
    for zz in (t, t + NT):
        @pl.when(zz != z)
        def _():
            greet(zdev(zz))

    @pl.when(is_root)
    def _():
        for k in range(NT):
            greet(at(wp, k))
        for k in range(1, NZ):
            greet(zdev((z + k) % NZ))

    ysend[...] = jnp.zeros_like(ysend)
    ysend[0:6, 0:RHS] = yl[0]
    ysend[8:14, 0:RHS] = yl[1]

    pl.semaphore_wait(barrier, jnp.where(is_root, 35, 13))

    to_next = pltpu.make_async_remote_copy(
        ysend, yall.at[NT + t], y_s.at[0], y_r.at[NT + t], at(wn, root_n), MESH
    )
    to_next.start()
    to_own = pltpu.make_async_remote_copy(
        ysend, yall.at[t], y_s.at[1], y_r.at[t], at(w, z % NT), MESH
    )

    @pl.when(jnp.logical_not(is_root))
    def _():
        to_own.start()

    @pl.when(is_root)
    def _():
        yall[t] = ysend[...]

    def cpiece(half, tt, k):
        return pltpu.make_async_remote_copy(
            cpk.at[half, tt],
            c48.at[half],
            c_s.at[half, k],
            c_r.at[half],
            at(w, tt),
            MESH,
        )

    for half, src in ((0, cs0), (1, cs1)):
        @pl.when(t == src)
        def _():
            pltpu.make_async_copy(ct.at[pl.ds(0, BAND)], cst.at[half], lsem.at[half]).wait()
            for zz in range(NZ):
                cpk[half, zz % NT, :, zz // NT * LANES : zz // NT * LANES + CK] = cst[
                    half, :, zz * CK : zz * CK + CK
                ]
            for tt in range(NT):
                for side in range(2):
                    cpk[half, tt, :, side * LANES + CK : (side + 1) * LANES] = jnp.zeros(
                        (BAND, LANES - CK), jnp.float32
                    )
            for k in range(1, NT):
                cpiece(half, (t + k) % NT, k).start()
            c48[half] = cpk[half, t]

    linv = lower_inverse(low[...])
    mi = lax.broadcasted_iota(jnp.int32, (CK, LANES), 0)
    pi = lax.broadcasted_iota(jnp.int32, (CK, LANES), 1)
    spread = jnp.where((mi == 6 * (pi // 8) + pi % 8) & (pi % 8 < 6), 1.0, 0.0)
    lpad = mm(linv, spread)
    rel = cmap[...] - w * BAND
    rel = jnp.where(rel < 0, rel + GK, rel)
    pt = jnp.where(rel == lax.broadcasted_iota(jnp.int32, (2 * BAND, CK), 0), 1.0, 0.0)
    g = mm(pt, lpad)
    gsec[...] = g[BAND:]

    send_g = pltpu.make_async_remote_copy(gsec, gprev, g_s, g_r, at(wn, root_n), MESH)

    @pl.when(t == root_n)
    def _():
        send_g.start()

    def zcopy(k):
        rows = pl.ds(pl.multiple_of(y * BAND, 8), BAND)
        return pltpu.make_async_remote_copy(
            gbuf.at[zh, rows], gbuf.at[zh, rows], z_s.at[k], z_r.at[zh], zdev((z + k) % NZ), MESH
        )

    @pl.when(is_root)
    def _():
        for k in range(2 * NT):
            @pl.when(k != t)
            def _():
                pltpu.make_async_remote_copy(
                    ysend, yall.at[k], y_s.at[1], y_r.at[k], at(w, t), MESH
                ).wait_recv()
        send_g.wait_recv()
        own = yall[0:NT].reshape(NT * 16, LANES)
        prev = yall[NT : 2 * NT].reshape(NT * 16, LANES)
        gs = mm(g[:BAND], own) + mm(gprev[...], prev)
        gbuf[zh, pl.ds(pl.multiple_of(y * BAND, 8), BAND), :] = gs
        for k in (8, 7, 9, 6, 10, 5, 11, 4, 12, 3, 13, 2, 14, 1, 15):
            zcopy(k).start()

    for half, src in ((0, cs0), (1, cs1)):
        @pl.when(t != src)
        def _():
            cpiece(half, t, 0).wait_recv()
    c2 = c48[...].reshape(2 * BAND, 2 * LANES)
    oper = mm(g, c2, ((0,), (0,)))

    def ycopy(h, k):
        rows = pl.ds(pl.multiple_of(y * BAND, 8), BAND)
        return pltpu.make_async_remote_copy(
            gbuf.at[h, rows], gbuf.at[h, rows], v_s.at[h, k], v_r.at[h, k], (z * NY + (y + k) % NY, t), MESH
        )

    def yrecv(h, k):
        rows = pl.ds(pl.multiple_of((y + NY - k) % NY * BAND, 8), BAND)
        return pltpu.make_async_remote_copy(
            gbuf.at[h, rows], gbuf.at[h, rows], v_s.at[h, k], v_r.at[h, k], (z * NY + (y + k) % NY, t), MESH
        )

    for h in range(2):
        @pl.when(jnp.logical_not(is_root & (zh == h)))
        def _():
            rows = pl.ds(pl.multiple_of(y * BAND, 8), BAND)
            pltpu.make_async_remote_copy(
                gbuf.at[h, rows], gbuf.at[h, rows], z_s.at[0], z_r.at[h], zdev((z + 1) % NZ), MESH
            ).wait_recv()
        for k in (2, 1, 3):
            ycopy(h, k).start()
    for h in range(2):
        for k in range(1, NY):
            yrecv(h, k).wait_recv()

    total = -mm(oper, gbuf[...].reshape(2 * LANES, LANES))
    part[...] = total.reshape(NT, 16, LANES)

    @pl.when(is_root)
    def _():
        own = yall[0:NT].reshape(NT * 16, LANES)
        part[...] += mm(lpad, mm(lpad, own), ((0,), (0,))).reshape(NT, 16, LANES)

    def dcopy(k):
        return pltpu.make_async_remote_copy(
            part.at[(t + k) % NT], crecv.at[k], d_s.at[k], d_r.at[k], at(w, (t + k) % NT), MESH
        )

    for k in (4, 3, 5, 2, 6, 1, 7):
        dcopy(k).start()
    acc = part[t]
    for k in range(1, NT):
        dcopy(k).wait_recv()
        acc += crecv[k]
    acc = acc.astype(out.dtype)
    out[0] = acc[0:6, 0:RHS]
    out[1] = acc[8:14, 0:RHS]

    to_next.wait_send()

    @pl.when(jnp.logical_not(is_root))
    def _():
        to_own.wait_send()

    for half, src in ((0, cs0), (1, cs1)):
        @pl.when(t == src)
        def _():
            for k in range(1, NT):
                cpiece(half, (t + k) % NT, k).wait_send()

    @pl.when(t == root_n)
    def _():
        send_g.wait_send()

    @pl.when(is_root)
    def _():
        for k in range(1, NZ):
            zcopy(k).wait_send()

    for h in range(2):
        for k in range(1, NY):
            ycopy(h, k).wait_send()
    for k in range(1, NT):
        dcopy(k).wait_send()


def coarse(yl, low, cmap, ct):
    vmem = pl.BlockSpec(memory_space=pltpu.VMEM)
    f32 = jnp.float32
    dma = pltpu.SemaphoreType.DMA
    return pl.pallas_call(
        coarse_kernel,
        out_shape=jax.ShapeDtypeStruct((2, 6, RHS), jnp.bfloat16),
        in_specs=[vmem, vmem, vmem, pl.BlockSpec(memory_space=pl.ANY)],
        out_specs=vmem,
        scratch_shapes=[
            pltpu.VMEM((16, LANES), f32),
            pltpu.VMEM((2 * NT, 16, LANES), f32),
            pltpu.VMEM((BAND, LANES), f32),
            pltpu.VMEM((BAND, LANES), f32),
            pltpu.VMEM((2, BAND, GK), f32),
            pltpu.VMEM((2, NT, BAND, 2 * LANES), f32),
            pltpu.VMEM((2, BAND, 2 * LANES), f32),
            pltpu.VMEM((2, LANES, LANES), f32),
            pltpu.VMEM((NT, 16, LANES), f32),
            pltpu.VMEM((NT, 16, LANES), f32),
            dma((2,)),
            dma((2,)), dma((2 * NT,)),
            dma, dma,
            dma((2, NT)), dma((2,)),
            dma((NZ,)), dma((2,)),
            dma((2, NY)), dma((2, NY)),
            dma((NT,)), dma((NT,)),
        ],
        compiler_params=pltpu.CompilerParams(collective_id=0, has_side_effects=True),
    )(yl, low, cmap, ct)


def per_device(duals, kernel, sub_counts, dual_sizes, cluster_factor, coarse_map, coarse_inverse):
    rhs_count, sub_count, dual_width = duals.shape
    position = lax.broadcasted_iota(jnp.int32, (sub_count, dual_width), 1)
    slot_index = lax.broadcasted_iota(jnp.int32, (sub_count, dual_width), 0)
    active = (position < dual_sizes[:, None]) & (slot_index < sub_counts[0])
    masked = jnp.where(active[:, None, :], kernel, jnp.zeros_like(kernel))
    local = jnp.einsum("rsi,ski->skr", duals, masked, preferred_element_type=jnp.float32)
    corr = coarse(local, cluster_factor[0], coarse_map, coarse_inverse.T)
    delta = jnp.einsum("skr,ski->rsi", corr, masked, preferred_element_type=jnp.float32)
    return (duals.astype(jnp.float32) - delta).astype(jnp.bfloat16)


def solution(mesh):
    in_specs = (
        P(None, ("wide", "clus"), None),
        P(("wide", "clus"), None, None),
        P(("wide", "clus")),
        P(("wide", "clus")),
        P("wide", None, None),
        P("wide", None),
        P(None, "clus"),
    )
    out_specs = P(None, ("wide", "clus"), None)
    return jax.shard_map(
        per_device, mesh=mesh, in_specs=in_specs, out_specs=out_specs, check_vma=False
    )
```

```python
import functools

import jax
import jax.numpy as jnp
from jax import lax
from jax.experimental import pallas as pl
from jax.experimental.pallas import tpu as pltpu
from jax.sharding import PartitionSpec as P

MESH = pl.DeviceIdType.MESH
NZ, NY, NT = 16, 4, 8
NW = NZ * NY
BAND = 24
GK = NW * BAND
CK = 96
RHS = 96
LANES = 128


def mm(a, b, dims=((1,), (0,))):
    return lax.dot_general(
        a, b, (dims, ((), ())), precision=lax.Precision.HIGHEST, preferred_element_type=jnp.float32
    )


def lower_inverse(lower):
    n = lower.shape[0]
    blocks = n // 8
    l3 = lower.reshape(blocks, 8, n)
    bi = lax.broadcasted_iota(jnp.int32, (blocks, 8, n), 0)
    ri = lax.broadcasted_iota(jnp.int32, (blocks, 8, n), 1)
    ci = lax.broadcasted_iota(jnp.int32, (blocks, 8, n), 2)
    own = ci - 8 * bi
    x = jnp.where(own == ri, 1.0, 0.0)
    rdiag = 1.0 / jnp.sum(jnp.where(own == ri, l3, 0.0), axis=2, keepdims=True)
    row = lax.broadcasted_iota(jnp.int32, (blocks, 8, 1), 1)
    for j in range(8):
        col = jnp.sum(jnp.where(own == j, l3, 0.0), axis=2, keepdims=True)
        pivot = x[:, j : j + 1, :] * rdiag[:, j : j + 1, :]
        x = jnp.where(row == j, pivot, x - jnp.where(row > j, col, 0.0) * pivot)
    x = x.reshape(n, n)
    r2 = lax.broadcasted_iota(jnp.int32, (n, n), 0)
    c2 = lax.broadcasted_iota(jnp.int32, (n, n), 1)
    size = 8
    while size < n:
        pair = 2 * size
        off = (r2 // pair == c2 // pair) & (r2 % pair >= size) & (c2 % pair < size)
        x = x - mm(x, mm(jnp.where(off, lower, 0.0), x))
        size = pair
    return x


def masked_rows(kern, count, size0, size1):
    rows = kern.reshape(12, kern.shape[-1])
    slot = lax.broadcasted_iota(jnp.int32, rows.shape, 0) % 2
    pos = lax.broadcasted_iota(jnp.int32, rows.shape, 1)
    limit = jnp.where(slot == 0, jnp.where(count > 0, size0, 0), jnp.where(count > 1, size1, 0))
    return jnp.where(pos < limit, rows.astype(jnp.float32), 0.0).astype(jnp.bfloat16)


def coarse_kernel(
    duals, kern, counts, sizes, low_in, cmap_in, ct, out,
    dbuf, kbuf, nbuf, sbuf, low, cmap,
    ysend, yall, gsec, gprev, cst, cpk, c48, gbuf, part, crecv,
    isem, lsem, y_s, y_r, g_s, g_r, c_s, c_r, z_s, z_r, v_s, v_r, d_s, d_r,
):
    w = lax.axis_index("wide")
    t = lax.axis_index("clus")
    z, y = w // NY, w % NY
    wn, wp = (w + 1) % NW, (w + NW - 1) % NW
    root_n = (wn // NY) % NT
    is_root = t == z % NT
    zh = z // NT
    cs0, cs1 = w // NT, wn // NT

    def at(ww, tt):
        return (ww, tt)

    def zdev(zz):
        return (zz * NY + y, t)

    gbuf[...] = jnp.zeros_like(gbuf)

    barrier = pltpu.get_barrier_semaphore()

    def greet(dev):
        pl.semaphore_signal(barrier, inc=1, device_id=dev, device_id_type=MESH)

    for zz in (t, t + NT):
        @pl.when(zz != z)
        def _():
            greet(zdev(zz))

    for k in range(1, NT):
        greet(at(w, (t + k) % NT))
    for k in range(1, NY):
        greet((z * NY + (y + k) % NY, t))

    @pl.when(is_root)
    def _():
        for k in range(NT):
            greet(at(wp, k))

    loads = [
        pltpu.make_async_copy(src, dst, isem.at[i])
        for i, (src, dst) in enumerate(
            ((kern, kbuf), (counts, nbuf), (sizes, sbuf), (duals, dbuf), (low_in, low), (cmap_in, cmap))
        )
    ]
    for load in loads:
        load.start()

    @pl.when(t == cs0)
    def _():
        pltpu.make_async_copy(
            ct.at[pl.ds(pl.multiple_of((w % NT) * BAND, 8), BAND)], cst.at[0], lsem.at[0]
        ).start()

    @pl.when(t == cs1)
    def _():
        pltpu.make_async_copy(
            ct.at[pl.ds(pl.multiple_of((wn % NT) * BAND, 8), BAND)], cst.at[1], lsem.at[1]
        ).start()

    ysend[...] = jnp.zeros_like(ysend)
    for load in loads[:4]:
        load.wait()
    masked = masked_rows(kbuf[...], nbuf[0], sbuf[0], sbuf[1]).reshape(6, 2, -1)
    local = lax.dot_general(
        masked, dbuf[...], (((2,), (2,)), ((1,), (1,))), preferred_element_type=jnp.float32
    )
    for slot in range(2):
        ysend[pl.ds(slot, 6, stride=2), 0:RHS] = local[slot]

    pl.semaphore_wait(barrier, jnp.where(is_root, 26, 11))

    to_next = pltpu.make_async_remote_copy(
        ysend, yall.at[NT + t], y_s.at[0], y_r.at[NT + t], at(wn, root_n), MESH
    )
    to_own = pltpu.make_async_remote_copy(
        ysend, yall.at[t], y_s.at[1], y_r.at[t], at(w, z % NT), MESH
    )
    to_next.start()

    @pl.when(jnp.logical_not(is_root))
    def _():
        to_own.start()

    @pl.when(is_root)
    def _():
        yall[t] = ysend[...]

    def cpiece(half, tt, k):
        return pltpu.make_async_remote_copy(
            cpk.at[half, tt],
            c48.at[half],
            c_s.at[half, k],
            c_r.at[half],
            at(w, tt),
            MESH,
        )

    for half, src in ((0, cs0), (1, cs1)):
        @pl.when(t == src)
        def _():
            pltpu.make_async_copy(ct.at[pl.ds(0, BAND)], cst.at[half], lsem.at[half]).wait()
            for zz in range(NZ):
                cpk[half, zz % NT, :, zz // NT * LANES : zz // NT * LANES + CK] = cst[
                    half, :, zz * CK : zz * CK + CK
                ]
            for tt in range(NT):
                for side in range(2):
                    cpk[half, tt, :, side * LANES + CK : (side + 1) * LANES] = jnp.zeros(
                        (BAND, LANES - CK), jnp.float32
                    )
            for k in range(1, NT):
                cpiece(half, (t + k) % NT, k).start()
            c48[half] = cpk[half, t]

    for load in loads[4:]:
        load.wait()
    linv = lower_inverse(low[...])
    mi = lax.broadcasted_iota(jnp.int32, (CK, LANES), 0)
    pi = lax.broadcasted_iota(jnp.int32, (CK, LANES), 1)
    slot_row = pi % 16
    spread = jnp.where(
        (mi == 12 * (pi // 16) + 6 * (slot_row % 2) + slot_row // 2) & (slot_row < 12), 1.0, 0.0
    )
    lpad = mm(linv, spread)
    rel = cmap[...] - w * BAND
    rel = jnp.where(rel < 0, rel + GK, rel)
    pt = jnp.where(rel == lax.broadcasted_iota(jnp.int32, (2 * BAND, CK), 0), 1.0, 0.0)
    g = mm(pt, lpad)
    gsec[...] = g[BAND:]

    send_g = pltpu.make_async_remote_copy(gsec, gprev, g_s, g_r, at(wn, root_n), MESH)

    @pl.when(t == root_n)
    def _():
        send_g.start()

    def zcopy(k):
        rows = pl.ds(pl.multiple_of(y * BAND, 8), BAND)
        return pltpu.make_async_remote_copy(
            gbuf.at[zh, rows], gbuf.at[zh, rows], z_s.at[k], z_r.at[zh], zdev((z + k) % NZ), MESH
        )

    @pl.when(is_root)
    def _():
        for k in range(2 * NT):
            @pl.when(k != t)
            def _():
                pltpu.make_async_remote_copy(
                    ysend, yall.at[k], y_s.at[1], y_r.at[k], at(w, t), MESH
                ).wait_recv()
        send_g.wait_recv()
        own = yall[0:NT].reshape(NT * 16, LANES)
        prev = yall[NT : 2 * NT].reshape(NT * 16, LANES)
        gs = mm(g[:BAND], own) + mm(gprev[...], prev)
        gbuf[zh, pl.ds(pl.multiple_of(y * BAND, 8), BAND), :] = gs
        for k in (8, 7, 9, 6, 10, 5, 11, 4, 12, 3, 13, 2, 14, 1, 15):
            zcopy(k).start()

    for half, src in ((0, cs0), (1, cs1)):
        @pl.when(t != src)
        def _():
            cpiece(half, t, 0).wait_recv()
    c2 = c48[...].reshape(2 * BAND, 2 * LANES)
    oper = mm(g, c2, ((0,), (0,)))

    def ycopy(h, k):
        rows = pl.ds(pl.multiple_of(y * BAND, 8), BAND)
        return pltpu.make_async_remote_copy(
            gbuf.at[h, rows], gbuf.at[h, rows], v_s.at[h, k], v_r.at[h, k], (z * NY + (y + k) % NY, t), MESH
        )

    def yrecv(h, k):
        rows = pl.ds(pl.multiple_of((y + NY - k) % NY * BAND, 8), BAND)
        return pltpu.make_async_remote_copy(
            gbuf.at[h, rows], gbuf.at[h, rows], v_s.at[h, k], v_r.at[h, k], (z * NY + (y + k) % NY, t), MESH
        )

    for h in range(2):
        @pl.when(jnp.logical_not(is_root & (zh == h)))
        def _():
            rows = pl.ds(pl.multiple_of(y * BAND, 8), BAND)
            pltpu.make_async_remote_copy(
                gbuf.at[h, rows], gbuf.at[h, rows], z_s.at[0], z_r.at[h], zdev((z + 1) % NZ), MESH
            ).wait_recv()
        for k in (2, 1, 3):
            ycopy(h, k).start()
    for h in range(2):
        for k in range(1, NY):
            yrecv(h, k).wait_recv()

    total = -mm(oper, gbuf[...].reshape(2 * LANES, LANES))
    part[...] = total.reshape(NT, 16, LANES)

    @pl.when(is_root)
    def _():
        own = yall[0:NT].reshape(NT * 16, LANES)
        part[...] += mm(lpad, mm(lpad, own), ((0,), (0,))).reshape(NT, 16, LANES)

    def dcopy(k):
        return pltpu.make_async_remote_copy(
            part.at[(t + k) % NT], crecv.at[k], d_s.at[k], d_r.at[k], at(w, (t + k) % NT), MESH
        )

    for k in (4, 3, 5, 2, 6, 1, 7):
        dcopy(k).start()
    acc = part[t]
    for k in range(1, NT):
        dcopy(k).wait_recv()
        acc += crecv[k]
    out[...] = acc.astype(out.dtype)

    to_next.wait_send()

    @pl.when(jnp.logical_not(is_root))
    def _():
        to_own.wait_send()

    for half, src in ((0, cs0), (1, cs1)):
        @pl.when(t == src)
        def _():
            for k in range(1, NT):
                cpiece(half, (t + k) % NT, k).wait_send()

    @pl.when(t == root_n)
    def _():
        send_g.wait_send()

    @pl.when(is_root)
    def _():
        for k in range(1, NZ):
            zcopy(k).wait_send()

    for h in range(2):
        for k in range(1, NY):
            ycopy(h, k).wait_send()
    for k in range(1, NT):
        dcopy(k).wait_send()


def coarse(duals, kern, counts, sizes, low, cmap, ct):
    hbm = pl.BlockSpec(memory_space=pl.ANY)
    f32 = jnp.float32
    dma = pltpu.SemaphoreType.DMA
    return pl.pallas_call(
        coarse_kernel,
        out_shape=jax.ShapeDtypeStruct((16, LANES), jnp.bfloat16),
        in_specs=[hbm] * 7,
        out_specs=pl.BlockSpec(memory_space=pltpu.VMEM),
        scratch_shapes=[
            pltpu.VMEM(duals.shape, duals.dtype),
            pltpu.VMEM(kern.shape, kern.dtype),
            pltpu.SMEM(counts.shape, jnp.int32),
            pltpu.SMEM(sizes.shape, jnp.int32),
            pltpu.VMEM(low.shape, f32),
            pltpu.VMEM(cmap.shape, jnp.int32),
            pltpu.VMEM((16, LANES), f32),
            pltpu.VMEM((2 * NT, 16, LANES), f32),
            pltpu.VMEM((BAND, LANES), f32),
            pltpu.VMEM((BAND, LANES), f32),
            pltpu.VMEM((2, BAND, GK), f32),
            pltpu.VMEM((2, NT, BAND, 2 * LANES), f32),
            pltpu.VMEM((2, BAND, 2 * LANES), f32),
            pltpu.VMEM((2, LANES, LANES), f32),
            pltpu.VMEM((NT, 16, LANES), f32),
            pltpu.VMEM((NT, 16, LANES), f32),
            dma((6,)),
            dma((2,)),
            dma((2,)), dma((2 * NT,)),
            dma, dma,
            dma((2, NT)), dma((2,)),
            dma((NZ,)), dma((2,)),
            dma((2, NY)), dma((2, NY)),
            dma((NT,)), dma((NT,)),
        ],
        compiler_params=pltpu.CompilerParams(collective_id=0, has_side_effects=True),
    )(duals, kern, counts, sizes, low, cmap, ct)


PIECES = 6


def project_kernel(duals, kern, counts, sizes, corr, out, obuf, sem):
    masked = masked_rows(kern[...], counts[0], sizes[0], sizes[1])
    rows = 2 * RHS
    pick = jnp.where(
        lax.broadcasted_iota(jnp.int32, (rows, LANES), 0) // 2
        == lax.broadcasted_iota(jnp.int32, (rows, LANES), 1),
        1.0,
        0.0,
    ).astype(jnp.bfloat16)
    wide = lax.dot_general(
        pick, corr[...], (((1,), (1,)), ((), ())), preferred_element_type=jnp.float32
    )
    same = (
        lax.broadcasted_iota(jnp.int32, wide.shape, 0) % 2
        == lax.broadcasted_iota(jnp.int32, wide.shape, 1) % 2
    )
    wide = jnp.where(same, wide, 0.0).astype(jnp.bfloat16)[:, :12]
    step = RHS // PIECES
    copies = []
    for i in range(PIECES):
        part = pl.ds(i * step, step)
        block = duals[part].reshape(2 * step, -1).astype(jnp.float32)
        delta = jnp.dot(
            wide[2 * step * i : 2 * step * (i + 1)], masked, preferred_element_type=jnp.float32
        )
        obuf[part] = (block - delta).astype(out.dtype).reshape(step, 2, -1)
        copy = pltpu.make_async_copy(obuf.at[part], out.at[part], sem.at[i])
        copy.start()
        copies.append(copy)
    for copy in copies:
        copy.wait()


def project(duals, kern, counts, sizes, corr):
    vmem = pl.BlockSpec(memory_space=pltpu.VMEM)
    smem = pl.BlockSpec(memory_space=pltpu.SMEM)
    return pl.pallas_call(
        project_kernel,
        out_shape=jax.ShapeDtypeStruct(duals.shape, duals.dtype),
        in_specs=[vmem, vmem, smem, smem, vmem],
        out_specs=pl.BlockSpec(memory_space=pl.ANY),
        scratch_shapes=[
            pltpu.VMEM(duals.shape, duals.dtype),
            pltpu.SemaphoreType.DMA((PIECES,)),
        ],
    )(duals, kern, counts, sizes, corr)


def per_device(duals, kernel, sub_counts, dual_sizes, cluster_factor, coarse_map, coarse_inverse):
    kern = kernel.transpose(1, 0, 2)
    corr = coarse(
        duals, kern, sub_counts, dual_sizes, cluster_factor[0], coarse_map, coarse_inverse.T
    )
    return project(duals, kern, sub_counts, dual_sizes, corr)


def solution(mesh):
    in_specs = (
        P(None, ("wide", "clus"), None),
        P(("wide", "clus"), None, None),
        P(("wide", "clus")),
        P(("wide", "clus")),
        P("wide", None, None),
        P("wide", None),
        P(None, "clus"),
    )
    out_specs = P(None, ("wide", "clus"), None)
    return jax.shard_map(
        per_device, mesh=mesh, in_specs=in_specs, out_specs=out_specs, check_vma=False
    )
```

```python
import functools

import jax
import jax.numpy as jnp
from jax import lax
from jax.experimental import pallas as pl
from jax.experimental.pallas import tpu as pltpu
from jax.sharding import PartitionSpec as P

MESH = pl.DeviceIdType.MESH
NZ, NY, NT = 16, 4, 8
NW = NZ * NY
BAND = 24
GK = NW * BAND
CK = 96
RHS = 96
LANES = 128
SPAN = CK + BAND


def mm(a, b, dims=((1,), (0,))):
    return lax.dot_general(
        a, b, (dims, ((), ())), precision=lax.Precision.HIGHEST, preferred_element_type=jnp.float32
    )


def lower_inverse(lower):
    n = lower.shape[0]
    blocks = n // 8
    l3 = lower.reshape(blocks, 8, n)
    bi = lax.broadcasted_iota(jnp.int32, (blocks, 8, n), 0)
    ri = lax.broadcasted_iota(jnp.int32, (blocks, 8, n), 1)
    ci = lax.broadcasted_iota(jnp.int32, (blocks, 8, n), 2)
    own = ci - 8 * bi
    x = jnp.where(own == ri, 1.0, 0.0)
    rdiag = 1.0 / jnp.sum(jnp.where(own == ri, l3, 0.0), axis=2, keepdims=True)
    row = lax.broadcasted_iota(jnp.int32, (blocks, 8, 1), 1)
    for j in range(8):
        col = jnp.sum(jnp.where(own == j, l3, 0.0), axis=2, keepdims=True)
        pivot = x[:, j : j + 1, :] * rdiag[:, j : j + 1, :]
        x = jnp.where(row == j, pivot, x - jnp.where(row > j, col, 0.0) * pivot)
    x = x.reshape(n, n)
    r2 = lax.broadcasted_iota(jnp.int32, (n, n), 0)
    c2 = lax.broadcasted_iota(jnp.int32, (n, n), 1)
    size = 8
    while size < n:
        pair = 2 * size
        off = (r2 // pair == c2 // pair) & (r2 % pair >= size) & (c2 % pair < size)
        x = x - mm(x, mm(jnp.where(off, lower, 0.0), x))
        size = pair
    return x


def masked_rows(kern, count, size0, size1):
    rows = kern.reshape(12, kern.shape[-1])
    slot = lax.broadcasted_iota(jnp.int32, rows.shape, 0) % 2
    pos = lax.broadcasted_iota(jnp.int32, rows.shape, 1)
    limit = jnp.where(slot == 0, jnp.where(count > 0, size0, 0), jnp.where(count > 1, size1, 0))
    return jnp.where(pos < limit, rows.astype(jnp.float32), 0.0).astype(jnp.bfloat16)


def coarse_kernel(
    duals, kern, counts, sizes, low_in, cmap_in, ct, out, dbuf, mbuf,
    kbuf, nbuf, sbuf, low, cmap,
    ysend, yall, cst, cpk, c48, blocks, part, crecv,
    isem, lsem, y_s, y_r, c_s, c_r, z_s, z_r, v_s, v_r, d_s, d_r,
):
    w = lax.axis_index("wide")
    t = lax.axis_index("clus")
    z, y = w // NY, w % NY
    wn = (w + 1) % NW
    is_root = t == z % NT
    zh = z // NT
    cs0, cs1 = w // NT, wn // NT

    def at(ww, tt):
        return (ww, tt)

    def zdev(zz):
        return (zz * NY + y, t)

    loads = [
        pltpu.make_async_copy(src, dst, isem.at[i])
        for i, (src, dst) in enumerate(
            ((kern, kbuf), (counts, nbuf), (sizes, sbuf), (duals, dbuf), (low_in, low), (cmap_in, cmap))
        )
    ]
    for load in loads:
        load.start()

    barrier = pltpu.get_barrier_semaphore()

    def greet(dev):
        pl.semaphore_signal(barrier, inc=1, device_id=dev, device_id_type=MESH)

    for zz in (t, t + NT):
        @pl.when(zz != z)
        def _():
            greet(zdev(zz))

    for k in range(1, NT):
        greet(at(w, (t + k) % NT))
    for k in range(1, NY):
        greet((z * NY + (y + k) % NY, t))

    @pl.when(t == cs0)
    def _():
        pltpu.make_async_copy(
            ct.at[pl.ds(pl.multiple_of((w % NT) * BAND, 8), BAND)], cst.at[0], lsem.at[0]
        ).start()

    @pl.when(t == cs1)
    def _():
        pltpu.make_async_copy(
            ct.at[pl.ds(pl.multiple_of((wn % NT) * BAND, 8), BAND)], cst.at[1], lsem.at[1]
        ).start()

    ysend[...] = jnp.zeros_like(ysend)
    for load in loads[:4]:
        load.wait()
    masked = masked_rows(kbuf[...], nbuf[0], sbuf[0], sbuf[1])
    mbuf[...] = masked
    masked = masked.reshape(6, 2, -1)
    local = lax.dot_general(
        masked, dbuf[...], (((2,), (2,)), ((1,), (1,))), preferred_element_type=jnp.float32
    )
    for slot in range(2):
        ysend[pl.ds(slot, 6, stride=2), 0:RHS] = local[slot]

    pl.semaphore_wait(barrier, jnp.where(is_root, 25, 10))

    to_own = pltpu.make_async_remote_copy(
        ysend, yall.at[t], y_s, y_r.at[t], at(w, z % NT), MESH
    )

    @pl.when(jnp.logical_not(is_root))
    def _():
        to_own.start()

    @pl.when(is_root)
    def _():
        yall[t] = ysend[...]

    def cpiece(half, tt, k):
        return pltpu.make_async_remote_copy(
            cpk.at[half, tt],
            c48.at[half],
            c_s.at[half, k],
            c_r.at[half],
            at(w, tt),
            MESH,
        )

    for half, src in ((0, cs0), (1, cs1)):
        @pl.when(t == src)
        def _():
            pltpu.make_async_copy(ct.at[pl.ds(0, BAND)], cst.at[half], lsem.at[half]).wait()
            for zz in range(NZ):
                at_lane = zz // NT * LANES
                if zz < NZ - 1:
                    cpk[half, zz % NT, :, at_lane : at_lane + SPAN] = cst[
                        half, :, zz * CK : zz * CK + SPAN
                    ]
                else:
                    cpk[half, zz % NT, :, at_lane : at_lane + CK] = cst[half, :, zz * CK :]
                    cpk[half, zz % NT, :, at_lane + CK : at_lane + SPAN] = cst[half, :, :BAND]
                cpk[half, zz % NT, :, at_lane + SPAN : at_lane + LANES] = jnp.zeros(
                    (BAND, LANES - SPAN), jnp.float32
                )
            for k in range(1, NT):
                cpiece(half, (t + k) % NT, k).start()
            c48[half] = cpk[half, t]

    for load in loads[4:]:
        load.wait()
    linv = lower_inverse(low[...])
    mi = lax.broadcasted_iota(jnp.int32, (CK, LANES), 0)
    pi = lax.broadcasted_iota(jnp.int32, (CK, LANES), 1)
    slot_row = pi % 16
    spread = jnp.where(
        (mi == 12 * (pi // 16) + 6 * (slot_row % 2) + slot_row // 2) & (slot_row < 12), 1.0, 0.0
    )
    lpad = mm(linv, spread)
    rel = cmap[...] - w * BAND
    rel = jnp.where(rel < 0, rel + GK, rel)
    pt = jnp.where(rel == lax.broadcasted_iota(jnp.int32, (2 * BAND, CK), 0), 1.0, 0.0)
    g = mm(pt, lpad)

    def zcopy(k):
        return pltpu.make_async_remote_copy(
            blocks.at[zh, y], blocks.at[zh, y], z_s.at[k], z_r.at[zh], zdev((z + k) % NZ), MESH
        )

    @pl.when(jnp.logical_not(is_root))
    def _():
        part[...] = jnp.zeros_like(part)

    @pl.when(is_root)
    def _():
        for k in range(NT):
            @pl.when(k != t)
            def _():
                pltpu.make_async_remote_copy(
                    ysend, yall.at[k], y_s, y_r.at[k], at(w, t), MESH
                ).wait_recv()
        own = yall[...].reshape(NT * 16, LANES)
        blocks[zh, y] = mm(g, own)
        for k in (8, 7, 9, 6, 10, 5, 11, 4, 12, 3, 13, 2, 14, 1, 15):
            zcopy(k).start()
        part[...] = mm(lpad, mm(lpad, own), ((0,), (0,))).reshape(NT, 16, LANES)

    for half, src in ((0, cs0), (1, cs1)):
        @pl.when(t != src)
        def _():
            cpiece(half, t, 0).wait_recv()
    c2 = c48[...].reshape(2 * BAND, 2 * LANES)
    oper = mm(g, c2, ((0,), (0,)))

    def ycopy(h, k):
        return pltpu.make_async_remote_copy(
            blocks.at[h, y], blocks.at[h, y], v_s.at[h, k], v_r.at[h, k], (z * NY + (y + k) % NY, t), MESH
        )

    def yrecv(h, k):
        return pltpu.make_async_remote_copy(
            blocks.at[h, y], blocks.at[h, (y + NY - k) % NY], v_s.at[h, k], v_r.at[h, k],
            (z * NY + (y + k) % NY, t), MESH,
        )

    for h in range(2):
        @pl.when(jnp.logical_not(is_root & (zh == h)))
        def _():
            pltpu.make_async_remote_copy(
                blocks.at[h, y], blocks.at[h, y], z_s.at[0], z_r.at[h], zdev((z + 1) % NZ), MESH
            ).wait_recv()
        for k in (2, 1, 3):
            ycopy(h, k).start()
    for h in range(2):
        for k in range(1, NY):
            yrecv(h, k).wait_recv()

    rows = []
    for h in range(2):
        rows.append(blocks[h, 0, :BAND])
        for yy in range(1, NY):
            rows.append(blocks[h, yy - 1, BAND:] + blocks[h, yy, :BAND])
        rows.append(blocks[h, NY - 1, BAND:])
        rows.append(jnp.zeros((LANES - SPAN, LANES), jnp.float32))
    part[...] -= mm(oper, jnp.concatenate(rows, axis=0)).reshape(NT, 16, LANES)

    def dcopy(k):
        return pltpu.make_async_remote_copy(
            part.at[(t + k) % NT], crecv.at[k], d_s.at[k], d_r.at[k], at(w, (t + k) % NT), MESH
        )

    for k in (4, 3, 5, 2, 6, 1, 7):
        dcopy(k).start()
    acc = part[t]
    for k in range(1, NT):
        dcopy(k).wait_recv()
        acc += crecv[k]
    out[...] = acc.astype(out.dtype)

    @pl.when(jnp.logical_not(is_root))
    def _():
        to_own.wait_send()

    for half, src in ((0, cs0), (1, cs1)):
        @pl.when(t == src)
        def _():
            for k in range(1, NT):
                cpiece(half, (t + k) % NT, k).wait_send()

    @pl.when(is_root)
    def _():
        for k in range(1, NZ):
            zcopy(k).wait_send()

    for h in range(2):
        for k in range(1, NY):
            ycopy(h, k).wait_send()
    for k in range(1, NT):
        dcopy(k).wait_send()


def coarse(duals, kern, counts, sizes, low, cmap, ct):
    hbm = pl.BlockSpec(memory_space=pl.ANY)
    f32 = jnp.float32
    dma = pltpu.SemaphoreType.DMA
    return pl.pallas_call(
        coarse_kernel,
        out_shape=[
            pltpu.VMEM((16, LANES), jnp.bfloat16),
            pltpu.VMEM(duals.shape, duals.dtype),
            pltpu.VMEM((12, duals.shape[2]), duals.dtype),
        ],
        in_specs=[hbm] * 7,
        out_specs=[pl.BlockSpec(memory_space=pltpu.VMEM)] * 3,
        scratch_shapes=[
            pltpu.VMEM(kern.shape, kern.dtype),
            pltpu.SMEM(counts.shape, jnp.int32),
            pltpu.SMEM(sizes.shape, jnp.int32),
            pltpu.VMEM(low.shape, f32),
            pltpu.VMEM(cmap.shape, jnp.int32),
            pltpu.VMEM((16, LANES), f32),
            pltpu.VMEM((NT, 16, LANES), f32),
            pltpu.VMEM((2, BAND, GK), f32),
            pltpu.VMEM((2, NT, BAND, 2 * LANES), f32),
            pltpu.VMEM((2, BAND, 2 * LANES), f32),
            pltpu.VMEM((2, NY, 2 * BAND, LANES), f32),
            pltpu.VMEM((NT, 16, LANES), f32),
            pltpu.VMEM((NT, 16, LANES), f32),
            dma((6,)),
            dma((2,)),
            dma, dma((NT,)),
            dma((2, NT)), dma((2,)),
            dma((NZ,)), dma((2,)),
            dma((2, NY)), dma((2, NY)),
            dma((NT,)), dma((NT,)),
        ],
        compiler_params=pltpu.CompilerParams(collective_id=0, has_side_effects=True),
    )(duals, kern, counts, sizes, low, cmap, ct)


PIECES = 6


def project_kernel(duals, masked_in, corr, out, obuf, sem):
    masked = masked_in[...]
    rows = 2 * RHS
    pick = jnp.where(
        lax.broadcasted_iota(jnp.int32, (rows, LANES), 0) // 2
        == lax.broadcasted_iota(jnp.int32, (rows, LANES), 1),
        1.0,
        0.0,
    ).astype(jnp.bfloat16)
    wide = lax.dot_general(
        pick, corr[...], (((1,), (1,)), ((), ())), preferred_element_type=jnp.float32
    )
    same = (
        lax.broadcasted_iota(jnp.int32, wide.shape, 0) % 2
        == lax.broadcasted_iota(jnp.int32, wide.shape, 1) % 2
    )
    wide = jnp.where(same, wide, 0.0).astype(jnp.bfloat16)[:, :12]
    step = RHS // PIECES
    copies = []
    for i in range(PIECES):
        part = pl.ds(i * step, step)
        block = duals[part].reshape(2 * step, -1).astype(jnp.float32)
        delta = jnp.dot(
            wide[2 * step * i : 2 * step * (i + 1)], masked, preferred_element_type=jnp.float32
        )
        obuf[part] = (block - delta).astype(out.dtype).reshape(step, 2, -1)
        copy = pltpu.make_async_copy(obuf.at[part], out.at[part], sem.at[i])
        copy.start()
        copies.append(copy)
    for copy in copies:
        copy.wait()


def project(duals, masked, corr):
    vmem = pl.BlockSpec(memory_space=pltpu.VMEM)
    return pl.pallas_call(
        project_kernel,
        out_shape=jax.ShapeDtypeStruct(duals.shape, duals.dtype),
        in_specs=[vmem, vmem, vmem],
        out_specs=pl.BlockSpec(memory_space=pl.ANY),
        scratch_shapes=[
            pltpu.VMEM(duals.shape, duals.dtype),
            pltpu.SemaphoreType.DMA((PIECES,)),
        ],
        compiler_params=pltpu.CompilerParams(vmem_limit_bytes=24 << 20),
    )(duals, masked, corr)


def per_device(duals, kernel, sub_counts, dual_sizes, cluster_factor, coarse_map, coarse_inverse):
    kern = kernel.transpose(1, 0, 2)
    corr, held, masked = coarse(
        duals, kern, sub_counts, dual_sizes, cluster_factor[0], coarse_map, coarse_inverse.T
    )
    return project(held, masked, corr)


def solution(mesh):
    in_specs = (
        P(None, ("wide", "clus"), None),
        P(("wide", "clus"), None, None),
        P(("wide", "clus")),
        P(("wide", "clus")),
        P("wide", None, None),
        P("wide", None),
        P(None, "clus"),
    )
    out_specs = P(None, ("wide", "clus"), None)
    return jax.shard_map(
        per_device, mesh=mesh, in_specs=in_specs, out_specs=out_specs, check_vma=False
    )
```

```python
import functools

import jax
import jax.numpy as jnp
from jax import lax
from jax.experimental import pallas as pl
from jax.experimental.pallas import tpu as pltpu
from jax.sharding import PartitionSpec as P

MESH = pl.DeviceIdType.MESH
NZ, NY, NT = 16, 4, 8
NW = NZ * NY
BAND = 24
GK = NW * BAND
CK = 96
RHS = 96
LANES = 128
SPAN = CK + BAND


def mm(a, b, dims=((1,), (0,))):
    return lax.dot_general(
        a, b, (dims, ((), ())), precision=lax.Precision.HIGHEST, preferred_element_type=jnp.float32
    )


def lower_inverse(lower):
    n = lower.shape[0]
    blocks = n // 8
    l3 = lower.reshape(blocks, 8, n)
    bi = lax.broadcasted_iota(jnp.int32, (blocks, 8, n), 0)
    ri = lax.broadcasted_iota(jnp.int32, (blocks, 8, n), 1)
    ci = lax.broadcasted_iota(jnp.int32, (blocks, 8, n), 2)
    own = ci - 8 * bi
    x = jnp.where(own == ri, 1.0, 0.0)
    rdiag = 1.0 / jnp.sum(jnp.where(own == ri, l3, 0.0), axis=2, keepdims=True)
    row = lax.broadcasted_iota(jnp.int32, (blocks, 8, 1), 1)
    for j in range(8):
        col = jnp.sum(jnp.where(own == j, l3, 0.0), axis=2, keepdims=True)
        pivot = x[:, j : j + 1, :] * rdiag[:, j : j + 1, :]
        x = jnp.where(row == j, pivot, x - jnp.where(row > j, col, 0.0) * pivot)
    x = x.reshape(n, n)
    r2 = lax.broadcasted_iota(jnp.int32, (n, n), 0)
    c2 = lax.broadcasted_iota(jnp.int32, (n, n), 1)
    size = 8
    while size < n:
        pair = 2 * size
        off = (r2 // pair == c2 // pair) & (r2 % pair >= size) & (c2 % pair < size)
        x = x - mm(x, mm(jnp.where(off, lower, 0.0), x))
        size = pair
    return x


def root_place(z):
    return 2 * (z % 4) + z // 4 % 2


def masked_rows(kern, count, size0, size1):
    rows = kern.reshape(12, kern.shape[-1])
    slot = lax.broadcasted_iota(jnp.int32, rows.shape, 0) % 2
    pos = lax.broadcasted_iota(jnp.int32, rows.shape, 1)
    limit = jnp.where(slot == 0, jnp.where(count > 0, size0, 0), jnp.where(count > 1, size1, 0))
    return jnp.where(pos < limit, rows.astype(jnp.float32), 0.0).astype(jnp.bfloat16)


def coarse_kernel(
    duals, kern, counts, sizes, low_in, cmap_in, ct, out, dbuf, mbuf,
    kbuf, nbuf, sbuf, low, cmap,
    ysend, yall, lpad, gop, oper, cst, cpk, c48, blocks, part, crecv,
    isem, lsem, y_s, y_r, c_s, c_r, z_s, z_r, v_s, v_r, d_s, d_r,
):
    w = lax.axis_index("wide")
    t = lax.axis_index("clus")
    z, y = w // NY, w % NY
    wn = (w + 1) % NW
    root = root_place(z)
    is_root = t == root
    z0 = t // 2 + 4 * (t % 2)
    zh = z // NT
    cs0, cs1 = w // NT, wn // NT

    def at(ww, tt):
        return (ww, tt)

    def zdev(zz):
        return (zz * NY + y, t)

    loads = [
        pltpu.make_async_copy(src, dst, isem.at[i])
        for i, (src, dst) in enumerate(
            ((kern, kbuf), (counts, nbuf), (sizes, sbuf), (duals, dbuf), (low_in, low), (cmap_in, cmap))
        )
    ]
    for load in loads:
        load.start()

    barrier = pltpu.get_barrier_semaphore()

    def greet(dev):
        pl.semaphore_signal(barrier, inc=1, device_id=dev, device_id_type=MESH)

    for zz in (z0, z0 + NT):
        @pl.when(zz != z)
        def _():
            greet(zdev(zz))

    for k in range(1, NT):
        greet(at(w, (t + k) % NT))
    for k in range(1, NY):
        greet((z * NY + (y + k) % NY, t))

    @pl.when(t == cs0)
    def _():
        pltpu.make_async_copy(
            ct.at[pl.ds(pl.multiple_of((w % NT) * BAND, 8), BAND)], cst.at[0], lsem.at[0]
        ).start()

    @pl.when(t == cs1)
    def _():
        pltpu.make_async_copy(
            ct.at[pl.ds(pl.multiple_of((wn % NT) * BAND, 8), BAND)], cst.at[1], lsem.at[1]
        ).start()

    def operators():
        for load in loads[4:]:
            load.wait()
        mi = lax.broadcasted_iota(jnp.int32, (CK, LANES), 0)
        pi = lax.broadcasted_iota(jnp.int32, (CK, LANES), 1)
        slot_row = pi % 16
        spread = jnp.where(
            (mi == 12 * (pi // 16) + 6 * (slot_row % 2) + slot_row // 2) & (slot_row < 12), 1.0, 0.0
        )
        linv = mm(lower_inverse(low[...]), spread)
        lpad[...] = linv
        rel = cmap[...] - w * BAND
        rel = jnp.where(rel < 0, rel + GK, rel)
        pt = jnp.where(rel == lax.broadcasted_iota(jnp.int32, (2 * BAND, CK), 0), 1.0, 0.0)
        gop[...] = mm(pt, linv)

    @pl.when(is_root)
    def _():
        operators()

    ysend[...] = jnp.zeros_like(ysend)
    for load in loads[:4]:
        load.wait()
    masked = masked_rows(kbuf[...], nbuf[0], sbuf[0], sbuf[1])
    mbuf[...] = masked
    masked = masked.reshape(6, 2, -1)
    local = lax.dot_general(
        masked, dbuf[...], (((2,), (2,)), ((1,), (1,))), preferred_element_type=jnp.float32
    )
    for slot in range(2):
        ysend[pl.ds(slot, 6, stride=2), 0:RHS] = local[slot]

    pl.semaphore_wait(barrier, jnp.where(is_root, 25, 10))

    to_own = pltpu.make_async_remote_copy(
        ysend, yall.at[t], y_s, y_r.at[t], at(w, root), MESH
    )

    @pl.when(jnp.logical_not(is_root))
    def _():
        to_own.start()

    @pl.when(is_root)
    def _():
        yall[t] = ysend[...]

    def cpiece(half, tt, k):
        return pltpu.make_async_remote_copy(
            cpk.at[half, tt],
            c48.at[half],
            c_s.at[half, k],
            c_r.at[half],
            at(w, tt),
            MESH,
        )

    for half, src in ((0, cs0), (1, cs1)):
        @pl.when(t == src)
        def _():
            pltpu.make_async_copy(ct.at[pl.ds(0, BAND)], cst.at[half], lsem.at[half]).wait()
            for zz in range(NZ):
                at_lane = zz // NT * LANES
                tt = root_place(zz)
                if zz < NZ - 1:
                    cpk[half, tt, :, at_lane : at_lane + SPAN] = cst[
                        half, :, zz * CK : zz * CK + SPAN
                    ]
                else:
                    cpk[half, tt, :, at_lane : at_lane + CK] = cst[half, :, zz * CK :]
                    cpk[half, tt, :, at_lane + CK : at_lane + SPAN] = cst[half, :, :BAND]
                cpk[half, tt, :, at_lane + SPAN : at_lane + LANES] = jnp.zeros(
                    (BAND, LANES - SPAN), jnp.float32
                )
            for k in range(1, NT):
                cpiece(half, (t + k) % NT, k).start()
            c48[half] = cpk[half, t]

    @pl.when(jnp.logical_not(is_root))
    def _():
        operators()

    def zcopy(k):
        return pltpu.make_async_remote_copy(
            blocks.at[zh, y], blocks.at[zh, y], z_s.at[k], z_r.at[zh], zdev((z + k) % NZ), MESH
        )

    @pl.when(jnp.logical_not(is_root))
    def _():
        part[...] = jnp.zeros_like(part)

    @pl.when(is_root)
    def _():
        for k in range(NT):
            @pl.when(k != t)
            def _():
                pltpu.make_async_remote_copy(
                    ysend, yall.at[k], y_s, y_r.at[k], at(w, t), MESH
                ).wait_recv()
        own = yall[...].reshape(NT * 16, LANES)
        blocks[zh, y] = mm(gop[...], own)
        for k in (8, 7, 9, 6, 10, 5, 11, 4, 12, 3, 13, 2, 14, 1, 15):
            zcopy(k).start()
        part[...] = mm(lpad[...], mm(lpad[...], own), ((0,), (0,))).reshape(NT, 16, LANES)

    for half, src in ((0, cs0), (1, cs1)):
        @pl.when(t != src)
        def _():
            cpiece(half, t, 0).wait_recv()
    c2 = c48[...].reshape(2 * BAND, 2 * LANES)
    both = mm(gop[...], c2, ((0,), (0,)))
    for h in range(2):
        oper[h] = both[:, h * LANES : (h + 1) * LANES]

    def ycopy(h, k):
        return pltpu.make_async_remote_copy(
            blocks.at[h, y], blocks.at[h, y], v_s.at[h, k], v_r.at[h, k], (z * NY + (y + k) % NY, t), MESH
        )

    def yrecv(h, k):
        return pltpu.make_async_remote_copy(
            blocks.at[h, y], blocks.at[h, (y + NY - k) % NY], v_s.at[h, k], v_r.at[h, k],
            (z * NY + (y + k) % NY, t), MESH,
        )

    away = (z + NZ - z0) % NZ
    near = jnp.where(jnp.minimum(away, NZ - away) <= NZ // 4, 0, 1)
    for h in (near, 1 - near):
        @pl.when(jnp.logical_not(is_root & (zh == h)))
        def _():
            pltpu.make_async_remote_copy(
                blocks.at[h, y], blocks.at[h, y], z_s.at[0], z_r.at[h], zdev((z + 1) % NZ), MESH
            ).wait_recv()
        for k in (2, 1, 3):
            ycopy(h, k).start()
    for h in (near, 1 - near):
        for k in range(1, NY):
            yrecv(h, k).wait_recv()
        rows = [blocks[h, 0, :BAND]]
        for yy in range(1, NY):
            rows.append(blocks[h, yy - 1, BAND:] + blocks[h, yy, :BAND])
        rows.append(blocks[h, NY - 1, BAND:])
        rows.append(jnp.zeros((LANES - SPAN, LANES), jnp.float32))
        part[...] -= mm(oper[h], jnp.concatenate(rows, axis=0)).reshape(NT, 16, LANES)

    def dcopy(k):
        return pltpu.make_async_remote_copy(
            part.at[(t + k) % NT], crecv.at[k], d_s.at[k], d_r.at[k], at(w, (t + k) % NT), MESH
        )

    for k in (4, 3, 5, 2, 6, 1, 7):
        dcopy(k).start()
    acc = part[t]
    for k in range(1, NT):
        dcopy(k).wait_recv()
        acc += crecv[k]
    out[...] = acc.astype(out.dtype)

    @pl.when(jnp.logical_not(is_root))
    def _():
        to_own.wait_send()

    for half, src in ((0, cs0), (1, cs1)):
        @pl.when(t == src)
        def _():
            for k in range(1, NT):
                cpiece(half, (t + k) % NT, k).wait_send()

    @pl.when(is_root)
    def _():
        for k in range(1, NZ):
            zcopy(k).wait_send()

    for h in range(2):
        for k in range(1, NY):
            ycopy(h, k).wait_send()
    for k in range(1, NT):
        dcopy(k).wait_send()


def coarse(duals, kern, counts, sizes, low, cmap, ct):
    hbm = pl.BlockSpec(memory_space=pl.ANY)
    f32 = jnp.float32
    dma = pltpu.SemaphoreType.DMA
    return pl.pallas_call(
        coarse_kernel,
        out_shape=[
            pltpu.VMEM((16, LANES), jnp.bfloat16),
            pltpu.VMEM(duals.shape, duals.dtype),
            pltpu.VMEM((12, duals.shape[2]), duals.dtype),
        ],
        in_specs=[hbm] * 7,
        out_specs=[pl.BlockSpec(memory_space=pltpu.VMEM)] * 3,
        scratch_shapes=[
            pltpu.VMEM(kern.shape, kern.dtype),
            pltpu.SMEM(counts.shape, jnp.int32),
            pltpu.SMEM(sizes.shape, jnp.int32),
            pltpu.VMEM(low.shape, f32),
            pltpu.VMEM(cmap.shape, jnp.int32),
            pltpu.VMEM((16, LANES), f32),
            pltpu.VMEM((NT, 16, LANES), f32),
            pltpu.VMEM((CK, LANES), f32),
            pltpu.VMEM((2 * BAND, LANES), f32),
            pltpu.VMEM((2, LANES, LANES), f32),
            pltpu.VMEM((2, BAND, GK), f32),
            pltpu.VMEM((2, NT, BAND, 2 * LANES), f32),
            pltpu.VMEM((2, BAND, 2 * LANES), f32),
            pltpu.VMEM((2, NY, 2 * BAND, LANES), f32),
            pltpu.VMEM((NT, 16, LANES), f32),
            pltpu.VMEM((NT, 16, LANES), f32),
            dma((6,)),
            dma((2,)),
            dma, dma((NT,)),
            dma((2, NT)), dma((2,)),
            dma((NZ,)), dma((2,)),
            dma((2, NY)), dma((2, NY)),
            dma((NT,)), dma((NT,)),
        ],
        compiler_params=pltpu.CompilerParams(collective_id=0, has_side_effects=True),
    )(duals, kern, counts, sizes, low, cmap, ct)


PIECES = 6


def project_kernel(duals, masked_in, corr, out, obuf, sem):
    masked = masked_in[...]
    rows = 2 * RHS
    pick = jnp.where(
        lax.broadcasted_iota(jnp.int32, (rows, LANES), 0) // 2
        == lax.broadcasted_iota(jnp.int32, (rows, LANES), 1),
        1.0,
        0.0,
    ).astype(jnp.bfloat16)
    wide = lax.dot_general(
        pick, corr[...], (((1,), (1,)), ((), ())), preferred_element_type=jnp.float32
    )
    same = (
        lax.broadcasted_iota(jnp.int32, wide.shape, 0) % 2
        == lax.broadcasted_iota(jnp.int32, wide.shape, 1) % 2
    )
    wide = jnp.where(same, wide, 0.0).astype(jnp.bfloat16)[:, :12]
    step = RHS // PIECES
    copies = []
    for i in range(PIECES):
        part = pl.ds(i * step, step)
        block = duals[part].reshape(2 * step, -1).astype(jnp.float32)
        delta = jnp.dot(
            wide[2 * step * i : 2 * step * (i + 1)], masked, preferred_element_type=jnp.float32
        )
        obuf[part] = (block - delta).astype(out.dtype).reshape(step, 2, -1)
        copy = pltpu.make_async_copy(obuf.at[part], out.at[part], sem.at[i])
        copy.start()
        copies.append(copy)
    for copy in copies:
        copy.wait()


def project(duals, masked, corr):
    vmem = pl.BlockSpec(memory_space=pltpu.VMEM)
    return pl.pallas_call(
        project_kernel,
        out_shape=jax.ShapeDtypeStruct(duals.shape, duals.dtype),
        in_specs=[vmem, vmem, vmem],
        out_specs=pl.BlockSpec(memory_space=pl.ANY),
        scratch_shapes=[
            pltpu.VMEM(duals.shape, duals.dtype),
            pltpu.SemaphoreType.DMA((PIECES,)),
        ],
        compiler_params=pltpu.CompilerParams(vmem_limit_bytes=24 << 20),
    )(duals, masked, corr)


def per_device(duals, kernel, sub_counts, dual_sizes, cluster_factor, coarse_map, coarse_inverse):
    kern = kernel.transpose(1, 0, 2)
    corr, held, masked = coarse(
        duals, kern, sub_counts, dual_sizes, cluster_factor[0], coarse_map, coarse_inverse.T
    )
    return project(held, masked, corr)


def solution(mesh):
    in_specs = (
        P(None, ("wide", "clus"), None),
        P(("wide", "clus"), None, None),
        P(("wide", "clus")),
        P(("wide", "clus")),
        P("wide", None, None),
        P("wide", None),
        P(None, "clus"),
    )
    out_specs = P(None, ("wide", "clus"), None)
    return jax.shard_map(
        per_device, mesh=mesh, in_specs=in_specs, out_specs=out_specs, check_vma=False
    )
```

```python
import functools

import jax
import jax.numpy as jnp
from jax import lax
from jax.experimental import pallas as pl
from jax.experimental.pallas import tpu as pltpu
from jax.sharding import PartitionSpec as P

MESH = pl.DeviceIdType.MESH
NZ, NY, NT = 16, 4, 8
NW = NZ * NY
BAND = 24
GK = NW * BAND
CK = 96
RHS = 96
LANES = 128
SPAN = CK + BAND


def mm(a, b, dims=((1,), (0,))):
    return lax.dot_general(
        a, b, (dims, ((), ())), precision=lax.Precision.HIGHEST, preferred_element_type=jnp.float32
    )


def lower_inverse(lower):
    n = lower.shape[0]
    blocks = n // 8
    l3 = lower.reshape(blocks, 8, n)
    bi = lax.broadcasted_iota(jnp.int32, (blocks, 8, n), 0)
    ri = lax.broadcasted_iota(jnp.int32, (blocks, 8, n), 1)
    ci = lax.broadcasted_iota(jnp.int32, (blocks, 8, n), 2)
    own = ci - 8 * bi
    x = jnp.where(own == ri, 1.0, 0.0)
    rdiag = 1.0 / jnp.sum(jnp.where(own == ri, l3, 0.0), axis=2, keepdims=True)
    row = lax.broadcasted_iota(jnp.int32, (blocks, 8, 1), 1)
    for j in range(8):
        col = jnp.sum(jnp.where(own == j, l3, 0.0), axis=2, keepdims=True)
        pivot = x[:, j : j + 1, :] * rdiag[:, j : j + 1, :]
        x = jnp.where(row == j, pivot, x - jnp.where(row > j, col, 0.0) * pivot)
    x = x.reshape(n, n)
    r2 = lax.broadcasted_iota(jnp.int32, (n, n), 0)
    c2 = lax.broadcasted_iota(jnp.int32, (n, n), 1)
    size = 8
    while size < n:
        pair = 2 * size
        off = (r2 // pair == c2 // pair) & (r2 % pair >= size) & (c2 % pair < size)
        x = x - mm(x, mm(jnp.where(off, lower, 0.0), x))
        size = pair
    return x


def root_place(z):
    x = z % 4
    return 2 * x + (z // 4 + 1 + (x + 1) // 2) % 2


def first_plane(t):
    x = t // 2
    return x + 4 * ((t + 1 + (x + 1) // 2) % 2)


def masked_rows(kern, count, size0, size1):
    rows = kern.reshape(12, kern.shape[-1])
    slot = lax.broadcasted_iota(jnp.int32, rows.shape, 0) % 2
    pos = lax.broadcasted_iota(jnp.int32, rows.shape, 1)
    limit = jnp.where(slot == 0, jnp.where(count > 0, size0, 0), jnp.where(count > 1, size1, 0))
    return jnp.where(pos < limit, rows.astype(jnp.float32), 0.0).astype(jnp.bfloat16)


def coarse_kernel(
    duals, kern, counts, sizes, low_in, cmap_in, ct, out, dbuf, mbuf,
    kbuf, nbuf, sbuf, low, cmap,
    ysend, yall, lpad, gop, oper, cst, cpk, c48, blocks, part, crecv,
    isem, lsem, y_s, y_r, c_s, c_r, z_s, z_r, v_s, v_r, d_s, d_r,
):
    w = lax.axis_index("wide")
    t = lax.axis_index("clus")
    z, y = w // NY, w % NY
    wn = (w + 1) % NW
    root = root_place(z)
    is_root = t == root
    z0 = first_plane(t)
    zh = z // NT
    cs0, cs1 = w // NT, wn // NT

    def at(ww, tt):
        return (ww, tt)

    def zdev(zz):
        return (zz * NY + y, t)

    barrier = pltpu.get_barrier_semaphore()

    def greet(dev):
        pl.semaphore_signal(barrier, inc=1, device_id=dev, device_id_type=MESH)

    for zz in (z0, z0 + NT):
        @pl.when(zz != z)
        def _():
            greet(zdev(zz))

    loads = [
        pltpu.make_async_copy(src, dst, isem.at[i])
        for i, (src, dst) in enumerate(
            ((duals, dbuf), (kern, kbuf), (counts, nbuf), (sizes, sbuf), (low_in, low), (cmap_in, cmap))
        )
    ]
    for load in loads:
        load.start()

    for k in range(1, NT):
        greet(at(w, (t + k) % NT))
    for k in range(1, NY):
        greet((z * NY + (y + k) % NY, t))

    @pl.when(t == cs0)
    def _():
        pltpu.make_async_copy(
            ct.at[pl.ds(pl.multiple_of((w % NT) * BAND, 8), BAND)], cst.at[0], lsem.at[0]
        ).start()

    @pl.when(t == cs1)
    def _():
        pltpu.make_async_copy(
            ct.at[pl.ds(pl.multiple_of((wn % NT) * BAND, 8), BAND)], cst.at[1], lsem.at[1]
        ).start()

    def operators():
        for load in loads[4:]:
            load.wait()
        mi = lax.broadcasted_iota(jnp.int32, (CK, LANES), 0)
        pi = lax.broadcasted_iota(jnp.int32, (CK, LANES), 1)
        slot_row = pi % 16
        spread = jnp.where(
            (mi == 12 * (pi // 16) + 6 * (slot_row % 2) + slot_row // 2) & (slot_row < 12), 1.0, 0.0
        )
        linv = mm(lower_inverse(low[...]), spread)
        lpad[...] = linv
        rel = cmap[...] - w * BAND
        rel = jnp.where(rel < 0, rel + GK, rel)
        pt = jnp.where(rel == lax.broadcasted_iota(jnp.int32, (2 * BAND, CK), 0), 1.0, 0.0)
        gop[...] = mm(pt, linv)

    @pl.when(is_root)
    def _():
        operators()

    ysend[...] = jnp.zeros_like(ysend)
    for load in loads[:4]:
        load.wait()
    masked = masked_rows(kbuf[...], nbuf[0], sbuf[0], sbuf[1])
    mbuf[...] = masked
    masked = masked.reshape(6, 2, -1)
    local = lax.dot_general(
        masked, dbuf[...], (((2,), (2,)), ((1,), (1,))), preferred_element_type=jnp.float32
    )
    for slot in range(2):
        ysend[pl.ds(slot, 6, stride=2), 0:RHS] = local[slot]

    pl.semaphore_wait(barrier, jnp.where(is_root, 25, 10))

    to_own = pltpu.make_async_remote_copy(
        ysend, yall.at[t], y_s, y_r.at[t], at(w, root), MESH
    )

    @pl.when(jnp.logical_not(is_root))
    def _():
        to_own.start()

    @pl.when(is_root)
    def _():
        yall[t] = ysend[...]

    def cpiece(half, tt, k):
        return pltpu.make_async_remote_copy(
            cpk.at[half, tt],
            c48.at[half],
            c_s.at[half, k],
            c_r.at[half],
            at(w, tt),
            MESH,
        )

    for half, src in ((0, cs0), (1, cs1)):
        @pl.when(t == src)
        def _():
            pltpu.make_async_copy(ct.at[pl.ds(0, BAND)], cst.at[half], lsem.at[half]).wait()
            for zz in range(NZ):
                at_lane = zz // NT * LANES
                tt = root_place(zz)
                if zz < NZ - 1:
                    cpk[half, tt, :, at_lane : at_lane + SPAN] = cst[
                        half, :, zz * CK : zz * CK + SPAN
                    ]
                else:
                    cpk[half, tt, :, at_lane : at_lane + CK] = cst[half, :, zz * CK :]
                    cpk[half, tt, :, at_lane + CK : at_lane + SPAN] = cst[half, :, :BAND]
                cpk[half, tt, :, at_lane + SPAN : at_lane + LANES] = jnp.zeros(
                    (BAND, LANES - SPAN), jnp.float32
                )
            for k in range(1, NT):
                cpiece(half, (t + k) % NT, k).start()
            c48[half] = cpk[half, t]

    @pl.when(jnp.logical_not(is_root))
    def _():
        operators()

    def ycopy(h, k):
        return pltpu.make_async_remote_copy(
            blocks.at[h, y], blocks.at[h, y], v_s.at[h, k], v_r.at[h, k], (z * NY + (y + k) % NY, t), MESH
        )

    def yrecv(h, k):
        return pltpu.make_async_remote_copy(
            blocks.at[h, y], blocks.at[h, (y + NY - k) % NY], v_s.at[h, k], v_r.at[h, k],
            (z * NY + (y + k) % NY, t), MESH,
        )

    def zcopy(zz):
        return pltpu.make_async_remote_copy(
            blocks.at[zh, y], blocks.at[zh, y], z_s.at[zz], z_r.at[zh], zdev(zz), MESH
        )

    @pl.when(jnp.logical_not(is_root))
    def _():
        part[...] = jnp.zeros_like(part)

    @pl.when(is_root)
    def _():
        for k in range(NT):
            @pl.when(k != t)
            def _():
                pltpu.make_async_remote_copy(
                    ysend, yall.at[k], y_s, y_r.at[k], at(w, t), MESH
                ).wait_recv()
        own = yall[...].reshape(NT * 16, LANES)
        blocks[zh, y] = mm(gop[...], own)
        for k in (2, 1, 3):
            ycopy(zh, k).start()
        for zz in (0, 1, 2, 3, 4, 5, 6, 7, 15, 14, 13, 12, 11, 10, 9, 8):
            @pl.when(zz != z)
            def _():
                zcopy(zz).start()
        part[...] = mm(lpad[...], mm(lpad[...], own), ((0,), (0,))).reshape(NT, 16, LANES)

    away = (z + NZ - z0) % NZ
    near = jnp.where(jnp.minimum(away, NZ - away) <= NZ // 4, 0, 1)
    def forward(h):
        @pl.when(jnp.logical_not(is_root & (zh == h)))
        def _():
            pltpu.make_async_remote_copy(
                blocks.at[h, y], blocks.at[h, y], z_s.at[0], z_r.at[h], zdev((z + 1) % NZ), MESH
            ).wait_recv()
            for k in (2, 1, 3):
                ycopy(h, k).start()

    forward(near)

    for half, src in ((0, cs0), (1, cs1)):
        @pl.when(t != src)
        def _():
            cpiece(half, t, 0).wait_recv()
    c2 = c48[...].reshape(2 * BAND, 2 * LANES)
    both = mm(gop[...], c2, ((0,), (0,)))
    for h in range(2):
        oper[h] = both[:, h * LANES : (h + 1) * LANES]

    forward(1 - near)

    for h in (near, 1 - near):
        for k in range(1, NY):
            yrecv(h, k).wait_recv()
        rows = [blocks[h, 0, :BAND]]
        for yy in range(1, NY):
            rows.append(blocks[h, yy - 1, BAND:] + blocks[h, yy, :BAND])
        rows.append(blocks[h, NY - 1, BAND:])
        rows.append(jnp.zeros((LANES - SPAN, LANES), jnp.float32))
        part[...] -= mm(oper[h], jnp.concatenate(rows, axis=0)).reshape(NT, 16, LANES)

    def dcopy(k):
        return pltpu.make_async_remote_copy(
            part.at[(t + k) % NT], crecv.at[k], d_s, d_r, at(w, (t + k) % NT), MESH
        )

    for k in (4, 3, 5, 2, 6, 1, 7):
        dcopy(k).start()
    @pl.when(jnp.logical_not(is_root))
    def _():
        to_own.wait_send()

    for half, src in ((0, cs0), (1, cs1)):
        @pl.when(t == src)
        def _():
            for k in range(1, NT):
                cpiece(half, (t + k) % NT, k).wait_send()

    @pl.when(is_root)
    def _():
        for zz in range(NZ):
            @pl.when(zz != z)
            def _():
                zcopy(zz).wait_send()

    for h in range(2):
        for k in range(1, NY):
            ycopy(h, k).wait_send()
    others = pl.ds(1, NT - 1)
    pieces = pltpu.make_async_remote_copy(
        crecv.at[others], crecv.at[others], d_s, d_r, at(w, (t + 1) % NT), MESH
    )
    pieces.wait_recv()
    acc = part[t] + jnp.sum(crecv[1:], axis=0)
    out[...] = acc.astype(out.dtype)

    pieces.wait_send()


def coarse(duals, kern, counts, sizes, low, cmap, ct):
    hbm = pl.BlockSpec(memory_space=pl.ANY)
    f32 = jnp.float32
    dma = pltpu.SemaphoreType.DMA
    return pl.pallas_call(
        coarse_kernel,
        out_shape=[
            pltpu.VMEM((16, LANES), jnp.bfloat16),
            pltpu.VMEM(duals.shape, duals.dtype),
            pltpu.VMEM((12, duals.shape[2]), duals.dtype),
        ],
        in_specs=[hbm] * 7,
        out_specs=[pl.BlockSpec(memory_space=pltpu.VMEM)] * 3,
        scratch_shapes=[
            pltpu.VMEM(kern.shape, kern.dtype),
            pltpu.SMEM(counts.shape, jnp.int32),
            pltpu.SMEM(sizes.shape, jnp.int32),
            pltpu.VMEM(low.shape, f32),
            pltpu.VMEM(cmap.shape, jnp.int32),
            pltpu.VMEM((16, LANES), f32),
            pltpu.VMEM((NT, 16, LANES), f32),
            pltpu.VMEM((CK, LANES), f32),
            pltpu.VMEM((2 * BAND, LANES), f32),
            pltpu.VMEM((2, LANES, LANES), f32),
            pltpu.VMEM((2, BAND, GK), f32),
            pltpu.VMEM((2, NT, BAND, 2 * LANES), f32),
            pltpu.VMEM((2, BAND, 2 * LANES), f32),
            pltpu.VMEM((2, NY, 2 * BAND, LANES), f32),
            pltpu.VMEM((NT, 16, LANES), f32),
            pltpu.VMEM((NT, 16, LANES), f32),
            dma((6,)),
            dma((2,)),
            dma, dma((NT,)),
            dma((2, NT)), dma((2,)),
            dma((NZ,)), dma((2,)),
            dma((2, NY)), dma((2, NY)),
            dma, dma,
        ],
        compiler_params=pltpu.CompilerParams(collective_id=0, has_side_effects=True),
    )(duals, kern, counts, sizes, low, cmap, ct)


PIECES = 6


def project_kernel(duals, masked_in, corr, out, obuf, sem):
    masked = masked_in[...]
    rows = 2 * RHS
    pick = jnp.where(
        lax.broadcasted_iota(jnp.int32, (rows, LANES), 0) // 2
        == lax.broadcasted_iota(jnp.int32, (rows, LANES), 1),
        1.0,
        0.0,
    ).astype(jnp.bfloat16)
    wide = lax.dot_general(
        pick, corr[...], (((1,), (1,)), ((), ())), preferred_element_type=jnp.float32
    )
    same = (
        lax.broadcasted_iota(jnp.int32, wide.shape, 0) % 2
        == lax.broadcasted_iota(jnp.int32, wide.shape, 1) % 2
    )
    wide = jnp.where(same, wide, 0.0).astype(jnp.bfloat16)[:, :12]
    step = RHS // PIECES
    copies = []
    for i in range(PIECES):
        part = pl.ds(i * step, step)
        block = duals[part].reshape(2 * step, -1).astype(jnp.float32)
        delta = jnp.dot(
            wide[2 * step * i : 2 * step * (i + 1)], masked, preferred_element_type=jnp.float32
        )
        obuf[part] = (block - delta).astype(out.dtype).reshape(step, 2, -1)
        copy = pltpu.make_async_copy(obuf.at[part], out.at[part], sem.at[i])
        copy.start()
        copies.append(copy)
    for copy in copies:
        copy.wait()


def project(duals, masked, corr):
    vmem = pl.BlockSpec(memory_space=pltpu.VMEM)
    return pl.pallas_call(
        project_kernel,
        out_shape=jax.ShapeDtypeStruct(duals.shape, duals.dtype),
        in_specs=[vmem, vmem, vmem],
        out_specs=pl.BlockSpec(memory_space=pl.ANY),
        scratch_shapes=[
            pltpu.VMEM(duals.shape, duals.dtype),
            pltpu.SemaphoreType.DMA((PIECES,)),
        ],
        compiler_params=pltpu.CompilerParams(vmem_limit_bytes=24 << 20),
    )(duals, masked, corr)


def per_device(duals, kernel, sub_counts, dual_sizes, cluster_factor, coarse_map, coarse_inverse):
    kern = kernel.transpose(1, 0, 2)
    corr, held, masked = coarse(
        duals, kern, sub_counts, dual_sizes, cluster_factor[0], coarse_map, coarse_inverse.T
    )
    return project(held, masked, corr)


def solution(mesh):
    in_specs = (
        P(None, ("wide", "clus"), None),
        P(("wide", "clus"), None, None),
        P(("wide", "clus")),
        P(("wide", "clus")),
        P("wide", None, None),
        P("wide", None),
        P(None, "clus"),
    )
    out_specs = P(None, ("wide", "clus"), None)
    return jax.shard_map(
        per_device, mesh=mesh, in_specs=in_specs, out_specs=out_specs, check_vma=False
    )
```

```python
import functools

import jax
import jax.numpy as jnp
from jax import lax
from jax.experimental import pallas as pl
from jax.experimental.pallas import tpu as pltpu
from jax.sharding import PartitionSpec as P

MESH = pl.DeviceIdType.MESH
NZ, NY, NT = 16, 4, 8
NW = NZ * NY
BAND = 24
GK = NW * BAND
CK = 96
RHS = 96
LANES = 128
SPAN = CK + BAND
CHUNKS = 3


def mm(a, b, dims=((1,), (0,))):
    return lax.dot_general(
        a, b, (dims, ((), ())), precision=lax.Precision.HIGHEST, preferred_element_type=jnp.float32
    )


def lower_inverse(lower):
    n = lower.shape[0]
    blocks = n // 8
    l3 = lower.reshape(blocks, 8, n)
    bi = lax.broadcasted_iota(jnp.int32, (blocks, 8, n), 0)
    ri = lax.broadcasted_iota(jnp.int32, (blocks, 8, n), 1)
    ci = lax.broadcasted_iota(jnp.int32, (blocks, 8, n), 2)
    own = ci - 8 * bi
    x = jnp.where(own == ri, 1.0, 0.0)
    rdiag = 1.0 / jnp.sum(jnp.where(own == ri, l3, 0.0), axis=2, keepdims=True)
    row = lax.broadcasted_iota(jnp.int32, (blocks, 8, 1), 1)
    for j in range(8):
        col = jnp.sum(jnp.where(own == j, l3, 0.0), axis=2, keepdims=True)
        pivot = x[:, j : j + 1, :] * rdiag[:, j : j + 1, :]
        x = jnp.where(row == j, pivot, x - jnp.where(row > j, col, 0.0) * pivot)
    x = x.reshape(n, n)
    r2 = lax.broadcasted_iota(jnp.int32, (n, n), 0)
    c2 = lax.broadcasted_iota(jnp.int32, (n, n), 1)
    size = 8
    while size < n:
        pair = 2 * size
        off = (r2 // pair == c2 // pair) & (r2 % pair >= size) & (c2 % pair < size)
        x = x - mm(x, mm(jnp.where(off, lower, 0.0), x))
        size = pair
    return x


def root_place(z):
    x = z % 4
    return 2 * x + (z // 4 + 1 + (x + 1) // 2) % 2


def first_plane(t):
    x = t // 2
    return x + 4 * ((t + 1 + (x + 1) // 2) % 2)


def masked_rows(kern, count, size0, size1):
    rows = kern.reshape(12, kern.shape[-1])
    slot = lax.broadcasted_iota(jnp.int32, rows.shape, 0) % 2
    pos = lax.broadcasted_iota(jnp.int32, rows.shape, 1)
    limit = jnp.where(slot == 0, jnp.where(count > 0, size0, 0), jnp.where(count > 1, size1, 0))
    return jnp.where(pos < limit, rows.astype(jnp.float32), 0.0).astype(jnp.bfloat16)


def coarse_kernel(
    duals, kern, counts, sizes, low_in, cmap_in, ct, out, dbuf, mbuf,
    kbuf, nbuf, sbuf, low, cmap,
    ysend, yall, lpad, gop, oper, cst, cpk, c48, blocks, part, crecv,
    isem, dsem, lsem, y_s, y_r, c_s, c_r, z_s, z_r, v_s, v_r, d_s, d_r,
):
    w = lax.axis_index("wide")
    t = lax.axis_index("clus")
    z, y = w // NY, w % NY
    wn = (w + 1) % NW
    root = root_place(z)
    is_root = t == root
    z0 = first_plane(t)
    zh = z // NT
    cs0, cs1 = w // NT, wn // NT

    def at(ww, tt):
        return (ww, tt)

    def zdev(zz):
        return (zz * NY + y, t)

    barrier = pltpu.get_barrier_semaphore()

    def greet(dev):
        pl.semaphore_signal(barrier, inc=1, device_id=dev, device_id_type=MESH)

    for zz in (z0, z0 + NT):
        @pl.when(zz != z)
        def _():
            greet(zdev(zz))

    loads = [
        pltpu.make_async_copy(src, dst, isem.at[i])
        for i, (src, dst) in enumerate(
            ((kern, kbuf), (counts, nbuf), (sizes, sbuf), (low_in, low), (cmap_in, cmap))
        )
    ]
    width = duals.shape[2] // CHUNKS
    chunks = [
        pltpu.make_async_copy(
            duals.at[:, :, pl.ds(i * width, width)], dbuf.at[:, :, pl.ds(i * width, width)], dsem.at[i]
        )
        for i in range(CHUNKS)
    ]
    for load in loads[:3] + chunks + loads[3:]:
        load.start()

    for k in range(1, NT):
        greet(at(w, (t + k) % NT))
    for k in range(1, NY):
        greet((z * NY + (y + k) % NY, t))

    @pl.when(t == cs0)
    def _():
        pltpu.make_async_copy(
            ct.at[pl.ds(pl.multiple_of((w % NT) * BAND, 8), BAND)], cst.at[0], lsem.at[0]
        ).start()

    @pl.when(t == cs1)
    def _():
        pltpu.make_async_copy(
            ct.at[pl.ds(pl.multiple_of((wn % NT) * BAND, 8), BAND)], cst.at[1], lsem.at[1]
        ).start()

    def operators():
        for load in loads[3:]:
            load.wait()
        mi = lax.broadcasted_iota(jnp.int32, (CK, LANES), 0)
        pi = lax.broadcasted_iota(jnp.int32, (CK, LANES), 1)
        slot_row = pi % 16
        spread = jnp.where(
            (mi == 12 * (pi // 16) + 6 * (slot_row % 2) + slot_row // 2) & (slot_row < 12), 1.0, 0.0
        )
        linv = mm(lower_inverse(low[...]), spread)
        lpad[...] = linv
        rel = cmap[...] - w * BAND
        rel = jnp.where(rel < 0, rel + GK, rel)
        pt = jnp.where(rel == lax.broadcasted_iota(jnp.int32, (2 * BAND, CK), 0), 1.0, 0.0)
        gop[...] = mm(pt, linv)

    @pl.when(is_root)
    def _():
        operators()

    ysend[...] = jnp.zeros_like(ysend)
    for load in loads[:3]:
        load.wait()
    masked = masked_rows(kbuf[...], nbuf[0], sbuf[0], sbuf[1])
    mbuf[...] = masked
    masked = masked.reshape(6, 2, -1)
    local = jnp.zeros((2, 6, RHS), jnp.float32)
    for i, chunk in enumerate(chunks):
        chunk.wait()
        cols = slice(i * width, (i + 1) * width)
        local += lax.dot_general(
            masked[:, :, cols],
            dbuf[:, :, cols],
            (((2,), (2,)), ((1,), (1,))),
            preferred_element_type=jnp.float32,
        )
    for slot in range(2):
        ysend[pl.ds(slot, 6, stride=2), 0:RHS] = local[slot]

    pl.semaphore_wait(barrier, jnp.where(is_root, 25, 10))

    to_own = pltpu.make_async_remote_copy(
        ysend, yall.at[t], y_s, y_r, at(w, root), MESH
    )

    @pl.when(jnp.logical_not(is_root))
    def _():
        to_own.start()

    @pl.when(is_root)
    def _():
        yall[t] = ysend[...]

    def cpiece(half, tt, k):
        return pltpu.make_async_remote_copy(
            cpk.at[half, tt],
            c48.at[half],
            c_s.at[half, k],
            c_r.at[half],
            at(w, tt),
            MESH,
        )

    for half, src in ((0, cs0), (1, cs1)):
        @pl.when(t == src)
        def _():
            pltpu.make_async_copy(ct.at[pl.ds(0, BAND)], cst.at[half], lsem.at[half]).wait()
            for zz in range(NZ):
                at_lane = zz // NT * LANES
                tt = root_place(zz)
                if zz < NZ - 1:
                    cpk[half, tt, :, at_lane : at_lane + SPAN] = cst[
                        half, :, zz * CK : zz * CK + SPAN
                    ]
                else:
                    cpk[half, tt, :, at_lane : at_lane + CK] = cst[half, :, zz * CK :]
                    cpk[half, tt, :, at_lane + CK : at_lane + SPAN] = cst[half, :, :BAND]
                cpk[half, tt, :, at_lane + SPAN : at_lane + LANES] = jnp.zeros(
                    (BAND, LANES - SPAN), jnp.float32
                )
            for k in range(1, NT):
                cpiece(half, (t + k) % NT, k).start()
            c48[half] = cpk[half, t]

    @pl.when(jnp.logical_not(is_root))
    def _():
        operators()

    def ycopy(h, k):
        return pltpu.make_async_remote_copy(
            blocks.at[h, y], blocks.at[h, y], v_s.at[h, k], v_r.at[h, k], (z * NY + (y + k) % NY, t), MESH
        )

    def yrecv(h, k):
        return pltpu.make_async_remote_copy(
            blocks.at[h, y], blocks.at[h, (y + NY - k) % NY], v_s.at[h, k], v_r.at[h, k],
            (z * NY + (y + k) % NY, t), MESH,
        )

    def ystart(h):
        for yy in range(NY):
            @pl.when(yy != y)
            def _():
                ycopy(h, (yy + NY - y) % NY).start()

    def zcopy(zz):
        return pltpu.make_async_remote_copy(
            blocks.at[zh, y], blocks.at[zh, y], z_s.at[zz], z_r.at[zh], zdev(zz), MESH
        )

    @pl.when(jnp.logical_not(is_root))
    def _():
        part[...] = jnp.zeros_like(part)

    @pl.when(is_root)
    def _():
        pltpu.make_async_remote_copy(
            yall.at[pl.ds(0, NT - 1)], yall.at[pl.ds(0, NT - 1)], y_s, y_r, at(w, t), MESH
        ).wait_recv()
        own = yall[...].reshape(NT * 16, LANES)
        blocks[zh, y] = mm(gop[...], own)
        def zstart(planes):
            for zz in planes:
                @pl.when(zz != z)
                def _():
                    zcopy(zz).start()

        zstart((0, 1, 2, 3))
        ystart(zh)
        zstart((4, 5, 6, 7, 15, 14, 13, 12, 11, 10, 9, 8))
        part[...] = mm(lpad[...], mm(lpad[...], own), ((0,), (0,))).reshape(NT, 16, LANES)

    away = (z + NZ - z0) % NZ
    near = jnp.where(jnp.minimum(away, NZ - away) <= NZ // 4, 0, 1)
    def forward(h):
        @pl.when(jnp.logical_not(is_root & (zh == h)))
        def _():
            pltpu.make_async_remote_copy(
                blocks.at[h, y], blocks.at[h, y], z_s.at[0], z_r.at[h], zdev((z + 1) % NZ), MESH
            ).wait_recv()
            ystart(h)

    forward(near)

    for half, src in ((0, cs0), (1, cs1)):
        @pl.when(t != src)
        def _():
            cpiece(half, t, 0).wait_recv()
    c2 = c48[...].reshape(2 * BAND, 2 * LANES)
    both = mm(gop[...], c2, ((0,), (0,)))
    for h in range(2):
        oper[h] = both[:, h * LANES : (h + 1) * LANES]

    forward(1 - near)

    for h in (near, 1 - near):
        for k in range(1, NY):
            yrecv(h, k).wait_recv()
        rows = [blocks[h, 0, :BAND]]
        for yy in range(1, NY):
            rows.append(blocks[h, yy - 1, BAND:] + blocks[h, yy, :BAND])
        rows.append(blocks[h, NY - 1, BAND:])
        rows.append(jnp.zeros((LANES - SPAN, LANES), jnp.float32))
        part[...] -= mm(oper[h], jnp.concatenate(rows, axis=0)).reshape(NT, 16, LANES)

    def dcopy(k):
        return pltpu.make_async_remote_copy(
            part.at[(t + k) % NT], crecv.at[k], d_s, d_r, at(w, (t + k) % NT), MESH
        )

    for tt in (1, 3, 2, 5, 4, 7, 6, 0):
        @pl.when(tt != t)
        def _():
            dcopy((tt + NT - t) % NT).start()

    @pl.when(jnp.logical_not(is_root))
    def _():
        to_own.wait_send()

    for half, src in ((0, cs0), (1, cs1)):
        @pl.when(t == src)
        def _():
            for k in range(1, NT):
                cpiece(half, (t + k) % NT, k).wait_send()

    @pl.when(is_root)
    def _():
        for zz in range(NZ):
            @pl.when(zz != z)
            def _():
                zcopy(zz).wait_send()

    for h in range(2):
        for k in range(1, NY):
            ycopy(h, k).wait_send()
    others = pl.ds(1, NT - 1)
    pieces = pltpu.make_async_remote_copy(
        crecv.at[others], crecv.at[others], d_s, d_r, at(w, (t + 1) % NT), MESH
    )
    pieces.wait_recv()
    acc = part[t] + jnp.sum(crecv[1:], axis=0)
    out[...] = acc.astype(out.dtype)

    pieces.wait_send()


def coarse(duals, kern, counts, sizes, low, cmap, ct):
    hbm = pl.BlockSpec(memory_space=pl.ANY)
    f32 = jnp.float32
    dma = pltpu.SemaphoreType.DMA
    return pl.pallas_call(
        coarse_kernel,
        out_shape=[
            pltpu.VMEM((16, LANES), jnp.bfloat16),
            pltpu.VMEM(duals.shape, duals.dtype),
            pltpu.VMEM((12, duals.shape[2]), duals.dtype),
        ],
        in_specs=[hbm] * 7,
        out_specs=[pl.BlockSpec(memory_space=pltpu.VMEM)] * 3,
        scratch_shapes=[
            pltpu.VMEM(kern.shape, kern.dtype),
            pltpu.SMEM(counts.shape, jnp.int32),
            pltpu.SMEM(sizes.shape, jnp.int32),
            pltpu.VMEM(low.shape, f32),
            pltpu.VMEM(cmap.shape, jnp.int32),
            pltpu.VMEM((16, LANES), f32),
            pltpu.VMEM((NT, 16, LANES), f32),
            pltpu.VMEM((CK, LANES), f32),
            pltpu.VMEM((2 * BAND, LANES), f32),
            pltpu.VMEM((2, LANES, LANES), f32),
            pltpu.VMEM((2, BAND, GK), f32),
            pltpu.VMEM((2, NT, BAND, 2 * LANES), f32),
            pltpu.VMEM((2, BAND, 2 * LANES), f32),
            pltpu.VMEM((2, NY, 2 * BAND, LANES), f32),
            pltpu.VMEM((NT, 16, LANES), f32),
            pltpu.VMEM((NT, 16, LANES), f32),
            dma((5,)),
            dma((CHUNKS,)),
            dma((2,)),
            dma, dma,
            dma((2, NT)), dma((2,)),
            dma((NZ,)), dma((2,)),
            dma((2, NY)), dma((2, NY)),
            dma, dma,
        ],
        compiler_params=pltpu.CompilerParams(collective_id=0, has_side_effects=True),
    )(duals, kern, counts, sizes, low, cmap, ct)


PIECES = 6


def project_kernel(duals, masked_in, corr, out, obuf, sem):
    masked = masked_in[...]
    rows = 2 * RHS
    pick = jnp.where(
        lax.broadcasted_iota(jnp.int32, (rows, LANES), 0) // 2
        == lax.broadcasted_iota(jnp.int32, (rows, LANES), 1),
        1.0,
        0.0,
    ).astype(jnp.bfloat16)
    wide = lax.dot_general(
        pick, corr[...], (((1,), (1,)), ((), ())), preferred_element_type=jnp.float32
    )
    same = (
        lax.broadcasted_iota(jnp.int32, wide.shape, 0) % 2
        == lax.broadcasted_iota(jnp.int32, wide.shape, 1) % 2
    )
    wide = jnp.where(same, wide, 0.0).astype(jnp.bfloat16)[:, :12]
    step = RHS // PIECES
    copies = []
    for i in range(PIECES):
        part = pl.ds(i * step, step)
        block = duals[part].reshape(2 * step, -1).astype(jnp.float32)
        delta = jnp.dot(
            wide[2 * step * i : 2 * step * (i + 1)], masked, preferred_element_type=jnp.float32
        )
        obuf[part] = (block - delta).astype(out.dtype).reshape(step, 2, -1)
        copy = pltpu.make_async_copy(obuf.at[part], out.at[part], sem.at[i])
        copy.start()
        copies.append(copy)
    for copy in copies:
        copy.wait()


def project(duals, masked, corr):
    vmem = pl.BlockSpec(memory_space=pltpu.VMEM)
    return pl.pallas_call(
        project_kernel,
        out_shape=jax.ShapeDtypeStruct(duals.shape, duals.dtype),
        in_specs=[vmem, vmem, vmem],
        out_specs=pl.BlockSpec(memory_space=pl.ANY),
        scratch_shapes=[
            pltpu.VMEM(duals.shape, duals.dtype),
            pltpu.SemaphoreType.DMA((PIECES,)),
        ],
        compiler_params=pltpu.CompilerParams(vmem_limit_bytes=24 << 20),
    )(duals, masked, corr)


def per_device(duals, kernel, sub_counts, dual_sizes, cluster_factor, coarse_map, coarse_inverse):
    kern = kernel.transpose(1, 0, 2)
    corr, held, masked = coarse(
        duals, kern, sub_counts, dual_sizes, cluster_factor[0], coarse_map, coarse_inverse.T
    )
    return project(held, masked, corr)


def solution(mesh):
    in_specs = (
        P(None, ("wide", "clus"), None),
        P(("wide", "clus"), None, None),
        P(("wide", "clus")),
        P(("wide", "clus")),
        P("wide", None, None),
        P("wide", None),
        P(None, "clus"),
    )
    out_specs = P(None, ("wide", "clus"), None)
    return jax.shard_map(
        per_device, mesh=mesh, in_specs=in_specs, out_specs=out_specs, check_vma=False
    )
```

```python
import functools

import jax
import jax.numpy as jnp
from jax import lax
from jax.experimental import pallas as pl
from jax.experimental.pallas import tpu as pltpu
from jax.sharding import PartitionSpec as P

MESH = pl.DeviceIdType.MESH
NZ, NY, NT = 16, 4, 8
NW = NZ * NY
BAND = 24
GK = NW * BAND
CK = 96
RHS = 96
LANES = 128
SPAN = CK + BAND
CHUNKS = 3


def mm(a, b, dims=((1,), (0,))):
    return lax.dot_general(
        a, b, (dims, ((), ())), precision=lax.Precision.HIGHEST, preferred_element_type=jnp.float32
    )


def mm_split(a, b):
    a_hi = a.astype(jnp.bfloat16)
    a_lo = (a - a_hi.astype(jnp.float32)).astype(jnp.bfloat16)
    b_hi = b.astype(jnp.bfloat16)
    b_lo = (b - b_hi.astype(jnp.float32)).astype(jnp.bfloat16)
    left = jnp.concatenate([a_hi, a_lo, a_hi], axis=1)
    right = jnp.concatenate([b_hi, b_hi, b_lo], axis=0)
    return jnp.dot(left, right, preferred_element_type=jnp.float32)


def lower_inverse(lower):
    n = lower.shape[0]
    blocks = n // 8
    l3 = lower.reshape(blocks, 8, n)
    bi = lax.broadcasted_iota(jnp.int32, (blocks, 8, n), 0)
    ri = lax.broadcasted_iota(jnp.int32, (blocks, 8, n), 1)
    ci = lax.broadcasted_iota(jnp.int32, (blocks, 8, n), 2)
    own = ci - 8 * bi
    x = jnp.where(own == ri, 1.0, 0.0)
    rdiag = 1.0 / jnp.sum(jnp.where(own == ri, l3, 0.0), axis=2, keepdims=True)
    row = lax.broadcasted_iota(jnp.int32, (blocks, 8, 1), 1)
    for j in range(8):
        col = jnp.sum(jnp.where(own == j, l3, 0.0), axis=2, keepdims=True)
        pivot = x[:, j : j + 1, :] * rdiag[:, j : j + 1, :]
        x = jnp.where(row == j, pivot, x - jnp.where(row > j, col, 0.0) * pivot)
    x = x.reshape(n, n)
    r2 = lax.broadcasted_iota(jnp.int32, (n, n), 0)
    c2 = lax.broadcasted_iota(jnp.int32, (n, n), 1)
    size = 8
    while size < n:
        pair = 2 * size
        off = (r2 // pair == c2 // pair) & (r2 % pair >= size) & (c2 % pair < size)
        x = x - mm(x, mm(jnp.where(off, lower, 0.0), x))
        size = pair
    return x


def root_place(z):
    x = z % 4
    return 2 * x + (z // 4 + 1 + (x + 1) // 2) % 2


def first_plane(t):
    x = t // 2
    return x + 4 * ((t + 1 + (x + 1) // 2) % 2)


def masked_rows(kern, count, size0, size1):
    rows = kern.reshape(12, kern.shape[-1])
    slot = lax.broadcasted_iota(jnp.int32, rows.shape, 0) % 2
    pos = lax.broadcasted_iota(jnp.int32, rows.shape, 1)
    limit = jnp.where(slot == 0, jnp.where(count > 0, size0, 0), jnp.where(count > 1, size1, 0))
    return jnp.where(pos < limit, rows.astype(jnp.float32), 0.0).astype(jnp.bfloat16)


def coarse_kernel(
    duals, kern, counts, sizes, low_in, cmap_in, ct, out, dbuf, mbuf,
    kbuf, nbuf, sbuf, low, cmap,
    ysend, yall, lpad, gop, oper, cst, cpk, c48, blocks, part, crecv,
    isem, dsem, lsem, y_s, y_r, c_s, c_r, z_s, z_r, v_s, v_r, d_s, d_r,
):
    w = lax.axis_index("wide")
    t = lax.axis_index("clus")
    z, y = w // NY, w % NY
    wn = (w + 1) % NW
    root = root_place(z)
    is_root = t == root
    z0 = first_plane(t)
    zh = z // NT
    cs0, cs1 = w // NT, wn // NT

    def at(ww, tt):
        return (ww, tt)

    def zdev(zz):
        return (zz * NY + y, t)

    barrier = pltpu.get_barrier_semaphore()

    def greet(dev):
        pl.semaphore_signal(barrier, inc=1, device_id=dev, device_id_type=MESH)

    for zz in (z0, z0 + NT):
        @pl.when(zz != z)
        def _():
            greet(zdev(zz))

    loads = [
        pltpu.make_async_copy(src, dst, isem.at[i])
        for i, (src, dst) in enumerate(
            ((kern, kbuf), (counts, nbuf), (sizes, sbuf), (low_in, low), (cmap_in, cmap))
        )
    ]
    width = duals.shape[2] // CHUNKS
    chunks = [
        pltpu.make_async_copy(
            duals.at[:, :, pl.ds(i * width, width)], dbuf.at[:, :, pl.ds(i * width, width)], dsem.at[i]
        )
        for i in range(CHUNKS)
    ]
    for load in loads[:3] + chunks + loads[3:]:
        load.start()

    for k in range(1, NT):
        greet(at(w, (t + k) % NT))
    for k in range(1, NY):
        greet((z * NY + (y + k) % NY, t))

    @pl.when(t == cs0)
    def _():
        pltpu.make_async_copy(
            ct.at[pl.ds(pl.multiple_of((w % NT) * BAND, 8), BAND)], cst.at[0], lsem.at[0]
        ).start()

    @pl.when(t == cs1)
    def _():
        pltpu.make_async_copy(
            ct.at[pl.ds(pl.multiple_of((wn % NT) * BAND, 8), BAND)], cst.at[1], lsem.at[1]
        ).start()

    def operators():
        for load in loads[3:]:
            load.wait()
        mi = lax.broadcasted_iota(jnp.int32, (CK, LANES), 0)
        pi = lax.broadcasted_iota(jnp.int32, (CK, LANES), 1)
        slot_row = pi % 16
        spread = jnp.where(
            (mi == 12 * (pi // 16) + 6 * (slot_row % 2) + slot_row // 2) & (slot_row < 12), 1.0, 0.0
        )
        linv = mm(lower_inverse(low[...]), spread)
        lpad[...] = linv
        rel = cmap[...] - w * BAND
        rel = jnp.where(rel < 0, rel + GK, rel)
        pt = jnp.where(rel == lax.broadcasted_iota(jnp.int32, (2 * BAND, CK), 0), 1.0, 0.0)
        gop[...] = mm(pt, linv)

    @pl.when(is_root)
    def _():
        operators()

    ysend[...] = jnp.zeros_like(ysend)
    for load in loads[:3]:
        load.wait()
    masked = masked_rows(kbuf[...], nbuf[0], sbuf[0], sbuf[1])
    mbuf[...] = masked
    masked = masked.reshape(6, 2, -1)
    local = jnp.zeros((2, 6, RHS), jnp.float32)
    for i, chunk in enumerate(chunks):
        chunk.wait()
        cols = slice(i * width, (i + 1) * width)
        local += lax.dot_general(
            masked[:, :, cols],
            dbuf[:, :, cols],
            (((2,), (2,)), ((1,), (1,))),
            preferred_element_type=jnp.float32,
        )
    for slot in range(2):
        ysend[pl.ds(slot, 6, stride=2), 0:RHS] = local[slot]

    pl.semaphore_wait(barrier, jnp.where(is_root, 25, 10))

    to_own = pltpu.make_async_remote_copy(
        ysend, yall.at[t], y_s, y_r, at(w, root), MESH
    )

    @pl.when(jnp.logical_not(is_root))
    def _():
        to_own.start()

    @pl.when(is_root)
    def _():
        yall[t] = ysend[...]

    def cpiece(half, tt, k):
        return pltpu.make_async_remote_copy(
            cpk.at[half, tt],
            c48.at[half],
            c_s.at[half, k],
            c_r.at[half],
            at(w, tt),
            MESH,
        )

    for half, src in ((0, cs0), (1, cs1)):
        @pl.when(t == src)
        def _():
            pltpu.make_async_copy(ct.at[pl.ds(0, BAND)], cst.at[half], lsem.at[half]).wait()
            for zz in range(NZ):
                at_lane = zz // NT * LANES
                tt = root_place(zz)
                if zz < NZ - 1:
                    cpk[half, tt, :, at_lane : at_lane + SPAN] = cst[
                        half, :, zz * CK : zz * CK + SPAN
                    ]
                else:
                    cpk[half, tt, :, at_lane : at_lane + CK] = cst[half, :, zz * CK :]
                    cpk[half, tt, :, at_lane + CK : at_lane + SPAN] = cst[half, :, :BAND]
                cpk[half, tt, :, at_lane + SPAN : at_lane + LANES] = jnp.zeros(
                    (BAND, LANES - SPAN), jnp.float32
                )
            for k in range(1, NT):
                cpiece(half, (t + k) % NT, k).start()
            c48[half] = cpk[half, t]

    @pl.when(jnp.logical_not(is_root))
    def _():
        operators()

    def ycopy(h, k):
        return pltpu.make_async_remote_copy(
            blocks.at[h, y], blocks.at[h, y], v_s.at[h, k], v_r.at[h, k], (z * NY + (y + k) % NY, t), MESH
        )

    def yrecv(h, k):
        return pltpu.make_async_remote_copy(
            blocks.at[h, y], blocks.at[h, (y + NY - k) % NY], v_s.at[h, k], v_r.at[h, k],
            (z * NY + (y + k) % NY, t), MESH,
        )

    def ystart(h):
        for yy in range(NY):
            @pl.when(yy != y)
            def _():
                ycopy(h, (yy + NY - y) % NY).start()

    def zcopy(zz):
        return pltpu.make_async_remote_copy(
            blocks.at[zh, y], blocks.at[zh, y], z_s.at[zz], z_r.at[zh], zdev(zz), MESH
        )

    @pl.when(jnp.logical_not(is_root))
    def _():
        part[...] = jnp.zeros_like(part)

    @pl.when(is_root)
    def _():
        pltpu.make_async_remote_copy(
            yall.at[pl.ds(0, NT - 1)], yall.at[pl.ds(0, NT - 1)], y_s, y_r, at(w, t), MESH
        ).wait_recv()
        own = yall[...].reshape(NT * 16, LANES)
        blocks[zh, y] = mm_split(gop[...], own)
        def zstart(planes):
            for zz in planes:
                @pl.when(zz != z)
                def _():
                    zcopy(zz).start()

        zstart((0, 1, 2, 3))
        ystart(zh)
        zstart((4, 5, 6, 7, 15, 14, 13, 12, 11, 10, 9, 8))
        part[...] = mm(lpad[...], mm(lpad[...], own), ((0,), (0,))).reshape(NT, 16, LANES)

    away = (z + NZ - z0) % NZ
    near = jnp.where(jnp.minimum(away, NZ - away) <= NZ // 4, 0, 1)
    def forward(h):
        @pl.when(jnp.logical_not(is_root & (zh == h)))
        def _():
            pltpu.make_async_remote_copy(
                blocks.at[h, y], blocks.at[h, y], z_s.at[0], z_r.at[h], zdev((z + 1) % NZ), MESH
            ).wait_recv()
            ystart(h)

    forward(near)

    for half, src in ((0, cs0), (1, cs1)):
        @pl.when(t != src)
        def _():
            cpiece(half, t, 0).wait_recv()
    c2 = c48[...].reshape(2 * BAND, 2 * LANES)
    both = mm(gop[...], c2, ((0,), (0,)))
    for h in range(2):
        oper[h] = both[:, h * LANES : (h + 1) * LANES]

    forward(1 - near)

    for h in (near, 1 - near):
        for k in range(1, NY):
            yrecv(h, k).wait_recv()
        rows = [blocks[h, 0, :BAND]]
        for yy in range(1, NY):
            rows.append(blocks[h, yy - 1, BAND:] + blocks[h, yy, :BAND])
        rows.append(blocks[h, NY - 1, BAND:])
        rows.append(jnp.zeros((LANES - SPAN, LANES), jnp.float32))
        part[...] -= mm_split(oper[h], jnp.concatenate(rows, axis=0)).reshape(NT, 16, LANES)

    def dcopy(k):
        return pltpu.make_async_remote_copy(
            part.at[(t + k) % NT], crecv.at[k], d_s, d_r, at(w, (t + k) % NT), MESH
        )

    for tt in (1, 3, 2, 5, 4, 7, 6, 0):
        @pl.when(tt != t)
        def _():
            dcopy((tt + NT - t) % NT).start()

    @pl.when(jnp.logical_not(is_root))
    def _():
        to_own.wait_send()

    for half, src in ((0, cs0), (1, cs1)):
        @pl.when(t == src)
        def _():
            for k in range(1, NT):
                cpiece(half, (t + k) % NT, k).wait_send()

    @pl.when(is_root)
    def _():
        for zz in range(NZ):
            @pl.when(zz != z)
            def _():
                zcopy(zz).wait_send()

    for h in range(2):
        for k in range(1, NY):
            ycopy(h, k).wait_send()
    others = pl.ds(1, NT - 1)
    pieces = pltpu.make_async_remote_copy(
        crecv.at[others], crecv.at[others], d_s, d_r, at(w, (t + 1) % NT), MESH
    )
    pieces.wait_recv()
    acc = part[t] + jnp.sum(crecv[1:], axis=0)
    out[...] = acc.astype(out.dtype)

    pieces.wait_send()


def coarse(duals, kern, counts, sizes, low, cmap, ct):
    hbm = pl.BlockSpec(memory_space=pl.ANY)
    f32 = jnp.float32
    dma = pltpu.SemaphoreType.DMA
    return pl.pallas_call(
        coarse_kernel,
        out_shape=[
            pltpu.VMEM((16, LANES), jnp.bfloat16),
            pltpu.VMEM(duals.shape, duals.dtype),
            pltpu.VMEM((12, duals.shape[2]), duals.dtype),
        ],
        in_specs=[hbm] * 7,
        out_specs=[pl.BlockSpec(memory_space=pltpu.VMEM)] * 3,
        scratch_shapes=[
            pltpu.VMEM(kern.shape, kern.dtype),
            pltpu.SMEM(counts.shape, jnp.int32),
            pltpu.SMEM(sizes.shape, jnp.int32),
            pltpu.VMEM(low.shape, f32),
            pltpu.VMEM(cmap.shape, jnp.int32),
            pltpu.VMEM((16, LANES), f32),
            pltpu.VMEM((NT, 16, LANES), f32),
            pltpu.VMEM((CK, LANES), f32),
            pltpu.VMEM((2 * BAND, LANES), f32),
            pltpu.VMEM((2, LANES, LANES), f32),
            pltpu.VMEM((2, BAND, GK), f32),
            pltpu.VMEM((2, NT, BAND, 2 * LANES), f32),
            pltpu.VMEM((2, BAND, 2 * LANES), f32),
            pltpu.VMEM((2, NY, 2 * BAND, LANES), f32),
            pltpu.VMEM((NT, 16, LANES), f32),
            pltpu.VMEM((NT, 16, LANES), f32),
            dma((5,)),
            dma((CHUNKS,)),
            dma((2,)),
            dma, dma,
            dma((2, NT)), dma((2,)),
            dma((NZ,)), dma((2,)),
            dma((2, NY)), dma((2, NY)),
            dma, dma,
        ],
        compiler_params=pltpu.CompilerParams(collective_id=0, has_side_effects=True),
    )(duals, kern, counts, sizes, low, cmap, ct)


PIECES = 6


def project_kernel(duals, masked_in, corr, out, obuf, sem):
    masked = masked_in[...]
    rows = 2 * RHS
    pick = jnp.where(
        lax.broadcasted_iota(jnp.int32, (rows, LANES), 0) // 2
        == lax.broadcasted_iota(jnp.int32, (rows, LANES), 1),
        1.0,
        0.0,
    ).astype(jnp.bfloat16)
    wide = lax.dot_general(
        pick, corr[...], (((1,), (1,)), ((), ())), preferred_element_type=jnp.float32
    )
    same = (
        lax.broadcasted_iota(jnp.int32, wide.shape, 0) % 2
        == lax.broadcasted_iota(jnp.int32, wide.shape, 1) % 2
    )
    wide = jnp.where(same, wide, 0.0).astype(jnp.bfloat16)[:, :12]
    step = RHS // PIECES
    copies = []
    for i in range(PIECES):
        part = pl.ds(i * step, step)
        block = duals[part].reshape(2 * step, -1).astype(jnp.float32)
        delta = jnp.dot(
            wide[2 * step * i : 2 * step * (i + 1)], masked, preferred_element_type=jnp.float32
        )
        obuf[part] = (block - delta).astype(out.dtype).reshape(step, 2, -1)
        copy = pltpu.make_async_copy(obuf.at[part], out.at[part], sem.at[i])
        copy.start()
        copies.append(copy)
    for copy in copies:
        copy.wait()


def project(duals, masked, corr):
    vmem = pl.BlockSpec(memory_space=pltpu.VMEM)
    return pl.pallas_call(
        project_kernel,
        out_shape=jax.ShapeDtypeStruct(duals.shape, duals.dtype),
        in_specs=[vmem, vmem, vmem],
        out_specs=pl.BlockSpec(memory_space=pl.ANY),
        scratch_shapes=[
            pltpu.VMEM(duals.shape, duals.dtype),
            pltpu.SemaphoreType.DMA((PIECES,)),
        ],
        compiler_params=pltpu.CompilerParams(vmem_limit_bytes=24 << 20),
    )(duals, masked, corr)


def per_device(duals, kernel, sub_counts, dual_sizes, cluster_factor, coarse_map, coarse_inverse):
    kern = kernel.transpose(1, 0, 2)
    corr, held, masked = coarse(
        duals, kern, sub_counts, dual_sizes, cluster_factor[0], coarse_map, coarse_inverse.T
    )
    return project(held, masked, corr)


def solution(mesh):
    in_specs = (
        P(None, ("wide", "clus"), None),
        P(("wide", "clus"), None, None),
        P(("wide", "clus")),
        P(("wide", "clus")),
        P("wide", None, None),
        P("wide", None),
        P(None, "clus"),
    )
    out_specs = P(None, ("wide", "clus"), None)
    return jax.shard_map(
        per_device, mesh=mesh, in_specs=in_specs, out_specs=out_specs, check_vma=False
    )
```
